256 devices in a mesh: ra: 32 (over x, z), dec: 4 (over y), band: 2 (over core).
Axes of the slice: x: 4, y: 4, z: 8, core: 2. Of those that a mesh axis runs over, the one named last changes fastest.
Arguments:
- morphology: bfloat16 [32, 4, 128, 4096], P('ra', 'dec'), may hold values from 0 to 1
- sed_amps: float32 [32, 4, 6, 128], P('ra', 'dec', 'band'), may hold values from 0.1 to 2
- slot_lists: int32 [32, 4, 5, 128], P('ra', 'dec'), may hold values from 0 to 16, as said below
- morph_step: float32 [32, 4, 128], P('ra', 'dec'), may hold values from 0.01 to 0.04
- sed_step: float32 [32, 4, 128], P('ra', 'dec'), may hold values from 9.765625e-06 to 3.90625e-05
- psf_kernels: bfloat16 [6, 32, 4096], P('band', 'ra'), may hold values from -0.75 to 0.75
- observed: bfloat16 [32, 4, 6, 16, 4096], P('ra', 'dec', 'band'), may hold values from -16 to 16
Outputs:
- morph_out: float32 [32, 4, 128, 4096], P('ra', 'dec', None, 'band')
- sed_out: float32 [32, 4, 6, 128], P('ra', 'dec', 'band')
The draws below stay inside these ranges and needn't reach their ends.
Inputs may be any that keep to these rules, and one draw needn't show every extreme that they name: `slot_lists`: in each home tile the sources 0 to some count - 1 are live (the count at least 32, and 128 in some tile); a live source has a slot below 16 in row 0; every other entry of a dead source is 16. No source lands beyond the declination edges. Each of rows 1 to 4 of a home tile holds at most 32 entries below 16, and some tile's row 1 holds exactly 32.
All inputs are finite; a program needn't handle non-finite values.
Results may differ from the reference program's by a relative error of at most 0.015.
Values may be sent and summed in bfloat16 or wider, within the bound.
A program may use at most 256 MiB of HBM per device.

```python
import math
import jax
import jax.numpy as jnp
from jax import lax

SIDE = 64
PIX = 4096
BANDS = 6
KERN = 32
SRC = 128
CAP = 32
SLOTS = 16
DIRS = 5
ITERS = 2
N_RA = 32
N_DEC = 4


def draw_slot_lists(key, part):
    key = jax.random.fold_in(key, 7)
    key_live, key_slot, key_over, key_full = jax.random.split(key, 4)
    tiles = N_RA * N_DEC
    live_count = jax.random.randint(key_live, (tiles,), SRC // 4, SRC + 1)
    full_tile = jax.random.randint(key_full, (), 0, tiles)
    tile_ids = jnp.arange(tiles)
    live_count = jnp.where(tile_ids == full_tile, SRC, live_count)
    alive = jnp.arange(SRC)[None, :] < live_count[:, None]
    slot_pick = jax.random.randint(key_slot, (tiles, DIRS, SRC), 0, SLOTS)
    intersections = jax.random.randint(key_over, (tiles, DIRS, SRC), 0, 10) < 3
    direction = jnp.arange(DIRS)
    forced = (tile_ids[:, None] == full_tile) & (direction[None, :] == 1)
    intersections = intersections | forced[:, :, None]
    dec_index = tile_ids % N_DEC
    edge_block = (direction[None, :] == 3) & (dec_index[:, None] == N_DEC - 1) | (direction[None, :] == 4) & (dec_index[:, None] == 0)
    candidate = alive[:, None, :] & intersections & (~edge_block)[:, :, None]
    rank = jnp.cumsum(candidate.astype(jnp.int32), axis=2)
    capped = candidate & (rank <= CAP)
    home_row = (direction == 0)[None, :, None]
    used = jnp.where(home_row, alive[:, None, :], capped)
    result = jnp.where(used, slot_pick, SLOTS)
    return result.reshape(N_RA, N_DEC, DIRS, SRC).astype(jnp.int32)


def levels(own_key, extent, shards, least, top_value):
    factor_of = 1.0
    for position, shards_of in shards:
        heights = jax.random.uniform(jax.random.fold_in(jax.random.fold_in(own_key, 6), position), (shards_of,), jnp.float32, least / len(shards), top_value / len(shards))
        factor_of = factor_of * jnp.repeat(jnp.exp(heights), extent[position] // shards_of).reshape((-1,) + (1,) * (len(extent) - 1 - position))
    return factor_of


def bell_draw(key, shape, width, reach, shards=(), held_as=jnp.bfloat16):
    drawn = width * jax.random.normal(key, shape, jnp.float32)
    if shards:
        drawn = drawn * levels(key, shape, shards, -0.22, 0.18)
    return jnp.clip(drawn, -reach, reach).astype(held_as)


def setup_inputs(seed: int = 0) -> dict:
    splits = jax.random.split(jax.random.key(seed), 8)
    morphology = jnp.clip(1.0 * jax.random.uniform(splits[0], (N_RA, N_DEC, SRC, PIX), jnp.float32) ** levels(splits[0], (N_RA, N_DEC, SRC, PIX), ((0, 32), (1, 4)), -0.2, 0.2), 0.0, 1.0).astype(jnp.bfloat16)
    sed_amps = jnp.clip(jnp.exp(math.log(2.0) - 2.9957323 * jax.random.uniform(splits[1], (N_RA, N_DEC, BANDS, SRC), jnp.float32) ** levels(splits[1], (N_RA, N_DEC, BANDS, SRC), ((0, 32), (1, 4), (2, 2)), -0.2, 0.2)), 0.1, 2.0)
    slot_lists = draw_slot_lists(jax.random.fold_in(splits[7], 71), 0)
    morph_step = jnp.clip(jnp.exp(math.log(0.04) - 1.3862944 * jax.random.uniform(splits[3], (N_RA, N_DEC, SRC), jnp.float32) ** levels(splits[3], (N_RA, N_DEC, SRC), ((0, 32), (1, 4)), -0.2, 0.2)), 0.01, 0.04)
    sed_step = jnp.clip(jnp.exp(math.log(3.9062499126885086e-05) - 1.3862944 * jax.random.uniform(splits[4], (N_RA, N_DEC, SRC), jnp.float32) ** levels(splits[4], (N_RA, N_DEC, SRC), ((0, 32), (1, 4)), -0.2, 0.2)), 9.765624781721272e-06, 3.9062499126885086e-05)
    psf_kernels = bell_draw(splits[5], (BANDS, KERN, PIX), SIDE ** -0.5, 0.75, ((0, 2), (1, 32)))
    observed = bell_draw(splits[6], (N_RA, N_DEC, BANDS, SLOTS, PIX), 3.0, 16.0, ((0, 32), (1, 4), (2, 2)))
    return dict(morphology=morphology, sed_amps=sed_amps, slot_lists=slot_lists, morph_step=morph_step, sed_step=sed_step, psf_kernels=psf_kernels, observed=observed)


def pick_kernels(psf_band, kern_index):
    selector = (kern_index[:, None] == jnp.arange(KERN, dtype=jnp.int32)[None, :]).astype(jnp.float32)
    picked = jnp.einsum('sk,bkp->bsp', selector, psf_band.astype(jnp.float32)).astype(jnp.bfloat16)
    return picked.reshape(picked.shape[0], picked.shape[1], SIDE, SIDE)


def convolve(morph_q, kernels):
    stamps = morph_q.reshape(morph_q.shape[0], SIDE, SIDE).astype(jnp.float32)
    kern_f = kernels.astype(jnp.float32)
    inner_prod = jnp.einsum('sij,bscj->bsic', stamps, kern_f).astype(jnp.bfloat16)
    convolved = jnp.einsum('bsai,bsic->bsac', kern_f, inner_prod.astype(jnp.float32))
    return convolved.reshape(convolved.shape[0], convolved.shape[1], SIDE * SIDE)


def partial_image(weighted, slot_row):
    selector = (slot_row[None, :] == jnp.arange(SLOTS, dtype=jnp.int32)[:, None]).astype(jnp.float32)
    return jnp.einsum('qs,bsp->bqp', selector, weighted, precision=lax.Precision.HIGHEST).astype(jnp.bfloat16)


def reference(morphology, sed_amps, slot_lists, morph_step, sed_step, psf_kernels, observed):
    tiles = N_RA * N_DEC
    flat_lists = slot_lists.reshape(tiles, DIRS, SRC)
    state_m = morphology.astype(jnp.float32).reshape(tiles, SRC, PIX)
    state_a = sed_amps.reshape(tiles, BANDS, SRC)
    eta_m = morph_step.reshape(tiles, SRC, 1)
    eta_a = sed_step.reshape(tiles, 1, SRC)
    obs_f = observed.astype(jnp.float32)
    tile_ids = jnp.arange(tiles, dtype=jnp.int32)
    for sweep in range(ITERS):
        morph_q = state_m.astype(jnp.bfloat16)
        sed_q = state_a.astype(jnp.bfloat16)

        def forward(tile_index):
            lists_here = flat_lists[tile_index]
            kernels = pick_kernels(psf_kernels, lists_here[0] % KERN)
            conv_here = convolve(morph_q[tile_index], kernels)
            weighted = sed_q[tile_index].astype(jnp.float32)[:, :, None] * conv_here
            return jnp.stack([partial_image(weighted, lists_here[direction]) for direction in range(DIRS)])

        images = lax.map(forward, tile_ids).reshape(N_RA, N_DEC, DIRS, BANDS, SLOTS, PIX)
        zero_row = jnp.zeros((N_RA, 1, BANDS, SLOTS, PIX), jnp.bfloat16)
        summed = images[:, :, 0].astype(jnp.float32)
        summed = summed + jnp.roll(images[:, :, 1], 1, axis=0).astype(jnp.float32)
        summed = summed + jnp.roll(images[:, :, 2], -1, axis=0).astype(jnp.float32)
        summed = summed + jnp.concatenate([zero_row, images[:, :-1, 3]], axis=1).astype(jnp.float32)
        summed = summed + jnp.concatenate([images[:, 1:, 4], zero_row], axis=1).astype(jnp.float32)
        residual = (summed - obs_f).astype(jnp.bfloat16)
        padded = jnp.concatenate([zero_row, residual, zero_row], axis=1)

        def backward(tile_index):
            ra_pos = tile_index // N_DEC
            dec_pos = tile_index % N_DEC + 1
            lists_here = flat_lists[tile_index]
            neighbours = [padded[ra_pos, dec_pos], padded[(ra_pos + 1) % N_RA, dec_pos],
                          padded[(ra_pos - 1) % N_RA, dec_pos], padded[ra_pos, dec_pos + 1],
                          padded[ra_pos, dec_pos - 1]]
            gathered = jnp.zeros((BANDS, SRC, PIX), jnp.float32)
            for direction in range(DIRS):
                selector = (lists_here[direction][None, :] == jnp.arange(SLOTS, dtype=jnp.int32)[:, None]).astype(jnp.float32)
                gathered = gathered + jnp.einsum('qs,bqp->bsp', selector, neighbours[direction].astype(jnp.float32))
            gathered_q = gathered.astype(jnp.bfloat16)
            kernels = pick_kernels(psf_kernels, lists_here[0] % KERN)
            conv_here = convolve(morph_q[tile_index], kernels)
            kern_f = kernels.astype(jnp.float32)
            res_stamps = gathered_q.astype(jnp.float32).reshape(BANDS, SRC, SIDE, SIDE)
            left_prod = jnp.einsum('bsai,bsac->bsic', kern_f, res_stamps).astype(jnp.bfloat16)
            back_prod = jnp.einsum('bsic,bscj->bsij', left_prod.astype(jnp.float32), kern_f)
            weights_here = sed_q[tile_index].astype(jnp.float32)[:, :, None, None]
            grad_m = jnp.sum(weights_here * back_prod, axis=0).reshape(SRC, PIX)
            grad_a = jnp.sum(conv_here * gathered_q.astype(jnp.float32), axis=2)
            return grad_m, grad_a

        grad_m, grad_a = lax.map(backward, tile_ids)
        state_m = jnp.maximum(state_m - eta_m * grad_m, 0.0)
        state_a = jnp.maximum(state_a - eta_a * grad_a, 0.0)
    return state_m.reshape(N_RA, N_DEC, SRC, PIX), state_a.reshape(N_RA, N_DEC, BANDS, SRC)
```

```python
import functools
import jax
import jax.numpy as jnp
from jax import lax
from jax.experimental import pallas as pl
from jax.experimental.pallas import tpu as pltpu
from jax.sharding import PartitionSpec as P

SIDE = 64
KERN = 32
ITERS = 2
SLOTS = 16
CAP = 32
SRC = 128
HALF = 2048
MESH = pl.DeviceIdType.MESH
F32 = jnp.float32
BF16 = jnp.bfloat16
I32 = jnp.int32


def lane_lo(rows):
    return lax.broadcasted_iota(I32, (rows, 128), 1) < SIDE


def swap(value):
    return pltpu.roll(value, SIDE, axis=1)


def block_diag(first, second):
    low = jnp.where(lane_lo(SIDE), 1.0, 0.0).astype(BF16)
    high = jnp.where(lane_lo(SIDE), 0.0, 1.0).astype(BF16)
    zero = jnp.zeros((SIDE, 128), BF16)
    return jnp.concatenate(
        [
            jnp.concatenate([first * low, zero], axis=1),
            jnp.concatenate([first * high, zero], axis=1),
            jnp.concatenate([zero, second], axis=1),
            jnp.concatenate([zero, zero], axis=1),
        ],
        axis=0,
    )


def dot(a, b):
    return jnp.dot(a, b, preferred_element_type=F32)


def turned(row):
    return jnp.broadcast_to(row, (SRC, SRC)).T


def places(row):
    source = lax.broadcasted_iota(I32, (1, SRC), 1)
    key_row = row * SRC + source
    column = turned(row)
    key_col = column * SRC + lax.broadcasted_iota(I32, (SRC, SRC), 0)
    rank = jnp.sum(jnp.where(key_col < key_row, 1, 0), axis=0, keepdims=True)
    below = jnp.sum(
        jnp.where(column < lax.broadcasted_iota(I32, (SRC, SRC), 1), 1, 0), axis=0, keepdims=True
    )
    return rank, below


def chosen(row, rank):
    entry = lax.broadcasted_iota(I32, (CAP, SRC), 0)
    return jnp.where(rank == entry, 1, 0) * jnp.where(row < SLOTS, 1, 0)


def to_stamps(parts, low_ref, high_ref, pair):
    x0, x1, x2 = parts
    mask = lane_lo(SLOTS)
    even, odd = pl.ds(2 * pair, SLOTS, stride=SIDE), pl.ds(2 * pair + 1, SLOTS, stride=SIDE)
    low_ref[even, :] = jnp.where(mask, x0, swap(x1))
    low_ref[odd, :] = jnp.where(mask, swap(x0), x1)
    high_ref[even, :] = jnp.where(mask, x2, 0.0)
    high_ref[odd, :] = jnp.where(mask, swap(x2), 0.0)


def deblend(
    n_ra, n_dec,
    morph, sed, lists, mstep, sstep, psf, obs,
    out_m, out_a,
    kp, k3, kt3, kst_lo, kst_hi,
    lists8, lists_in, amps, amps_in, amp_now,
    pick_out, pick_back, home_amp, home_back, step_col, entries, table,
    mq, mf, vout, vin, xs, s_lo, s_hi, o_lo, o_hi, zs, pfx, model, resid,
    b_lo, b_hi, bflat, gs, gflat, gsum, gin, gret, hown, hsend, hin,
    arep, ga_rows, ga_send, ga_ret, ga_home,
    psf_send, psf_recv, list_sem, amp_sem, vis_sem, fwd_sem, mine_sem, home_sem,
    part_sem, back_sem, gain_sem, table_sem,
):
    r = lax.axis_index("ra")
    c = lax.axis_index("dec")
    b = lax.axis_index("band")
    other = 1 - b
    right, left = lax.rem(r + 1, n_ra), lax.rem(r + n_ra - 1, n_ra)
    up, down = lax.rem(c + 1, n_dec), lax.rem(c + n_dec - 1, n_dec)
    target = [(right, c, b), (left, c, b), (r, up, b), (r, down, b)]
    origin = [(left, c, b), (right, c, b), (r, down, b), (r, up, b)]
    sibling = (r, c, other)
    nk = min(SLOTS, n_ra)

    def send(src, dst, sems, index, device):
        return pltpu.make_async_remote_copy(
            src_ref=src, dst_ref=dst,
            send_sem=sems.at[(0,) + index], recv_sem=sems.at[(1,) + index],
            device_id=device, device_id_type=MESH,
        )

    barrier = pltpu.get_barrier_semaphore()

    def greet(step, carry):
        pl.semaphore_signal(
            barrier, inc=1, device_id=(lax.rem(r + step, n_ra), c, b), device_id_type=MESH
        )
        return carry

    lax.fori_loop(1, n_ra, greet, 0)
    for device in target[2:] + [sibling]:
        pl.semaphore_signal(barrier, inc=1, device_id=device, device_id_type=MESH)
    lists8[...] = jnp.full((8, SRC), SLOTS, I32)
    lists8[0:5, :] = lists[...]
    amp_now[...] = jnp.zeros((8, SRC), F32)
    amp_now[0:3, :] = sed[...]
    amps[0] = amp_now[...].astype(BF16).astype(F32)
    pl.semaphore_wait(barrier, n_ra - 1 + 3)

    list_copies = [
        send(lists8, lists_in.at[d], list_sem, (d,), target[d]) for d in range(4)
    ]
    for copy in list_copies:
        copy.start()

    def psf_copy(step):
        return pltpu.make_async_remote_copy(
            src_ref=psf, dst_ref=kp.at[lax.rem(r, SLOTS)],
            send_sem=psf_send.at[step], recv_sem=psf_recv.at[lax.rem(r, SLOTS)],
            device_id=(lax.rem(r + step, n_ra), c, b), device_id_type=MESH,
        )

    def spread_psf():
        def body(step, carry):
            psf_copy(step).start()
            return carry

        lax.fori_loop(1, n_ra, body, 0)
        kp[lax.rem(r, SLOTS)] = psf[...]

    def amp_copy(it, d):
        return send(amps.at[it], amps_in.at[it, d], amp_sem, (it, d), target[d])

    def vis_copy(it, d):
        rows = pl.ds(CAP * d, CAP)
        return send(vout.at[it, rows], vin.at[it, b, rows], vis_sem, (it, d), target[d])

    def fwd_copy(it, d, half):
        rows = pl.ds(CAP * d, CAP)
        return send(vin.at[it, half, rows], vin.at[it, half, rows], fwd_sem, (it, d), sibling)

    def mine_copy(half):
        return send(mq.at[1, half], mq.at[1, half], mine_sem, (0,), sibling)

    def home_copy(it):
        return send(hsend.at[it], hin.at[it], home_sem, (it,), sibling)

    def part_copy(it, d, half):
        rows = pl.ds(CAP * d, CAP)
        return send(gflat.at[it, half, rows], gin.at[it, rows], part_sem, (it, d), sibling)

    def back_copy(it, d):
        rows = pl.ds(CAP * d, CAP)
        return send(gsum.at[it, rows], gret.at[it, rows], back_sem, (it, d), origin[d])

    def gain_copy(it, d):
        return send(ga_send.at[it], ga_ret.at[it, d], gain_sem, (it, d), origin[d])

    for d in range(4):
        amp_copy(0, d).start()

    for d in range(4):
        row = lists8[d + 1 : d + 2, :]
        rank, _ = places(row)
        entries[pl.ds(CAP * d, CAP), :] = chosen(row, rank)
    pick = entries[...].astype(F32)
    pick_out[...] = pick
    pick_back[...] = pick.T.astype(BF16)

    mq[0, 0] = morph[:, 0:HALF]
    mq[0, 1] = morph[:, HALF : 2 * HALF]
    mf[...] = mq[0, b].astype(F32)

    def send_visitors(it):
        def body(j, carry):
            cols = pl.ds(pl.multiple_of(j * 256, 256), 256)
            vout[it, :, cols] = dot(pick_out[...].astype(BF16), mq[it, b, :, cols]).astype(BF16)
            return carry

        lax.fori_loop(0, HALF // 256, body, 0)
        for d in range(4):
            vis_copy(it, d).start()

    send_visitors(0)

    @pl.when(r < SLOTS)
    def _():
        spread_psf()

    if nk < SLOTS:
        kp[nk:SLOTS] = jnp.zeros((SLOTS - nk, 96, 128), BF16)

    step_col[...] = turned(mstep[...])
    slot0 = lists8[0:1, :]
    is_slot = jnp.where(slot0 == lax.broadcasted_iota(I32, (SLOTS, SRC), 0), 1.0, 0.0)
    bflat[...] = jnp.zeros(bflat.shape, BF16)
    pfx[0] = jnp.zeros((SIDE, 256), F32)
    pfx[65] = jnp.zeros((SIDE, 256), F32)

    for half in range(2):
        def obs_body(j, carry, half=half):
            cols = pl.ds(pl.multiple_of((half * 16 + j) * 128, 128), 128)
            parts = [obs[band, :, cols].astype(F32) for band in range(3)]
            to_stamps(parts, o_lo, o_hi, half * 16 + j)
            return carry

        lax.fori_loop(0, 16, obs_body, 0)

    def take_lists():
        table[...] = jnp.zeros((8, SRC), I32)
        for d in range(4):
            list_copies[d].wait_recv()
            row = lists_in[d, d + 1 : d + 2, :]
            rank, below = places(row)
            picked = chosen(row, rank)
            entries[pl.ds(CAP * d, CAP), :] = picked
            table[d + 2 : d + 3, :] = jnp.minimum(below, CAP)
        first, second = [], []
        for d in range(4):
            picked = entries[pl.ds(CAP * d, CAP), :]
            first.append(picked * lists_in[d, 0:1, :])
            second.append(picked * lists_in[d, d + 1 : d + 2, :])
        table[0:1, :] = jnp.minimum(
            jnp.sum(jnp.concatenate(first, axis=0).T, axis=0, keepdims=True), SLOTS - 1
        )
        table[1:2, :] = jnp.minimum(
            jnp.sum(jnp.concatenate(second, axis=0).T, axis=0, keepdims=True), SLOTS - 1
        )

    take_lists()

    def with_table(smem):
        copy = pltpu.make_async_copy(table, smem, table_sem)
        copy.start()
        copy.wait()
        for it in range(ITERS):
            one_iteration(it, smem)

    def home_weights(it):
        rows = [is_slot * amps[it, band : band + 1, :] for band in range(3)]
        full = jnp.concatenate(rows + [jnp.zeros((SRC - 48, SRC), F32)], axis=0)
        home_amp[...] = full[0:48].astype(BF16)
        home_back[...] = full.T.astype(BF16)

    def unpack(k):
        mask = lane_lo(SIDE)
        p01 = kp[k, 0:SIDE, :].astype(F32)
        fold = kp[k, SIDE:96, :].astype(F32)
        mask32 = lane_lo(32)
        p2 = jnp.concatenate(
            [jnp.where(mask32, fold, 0.0), jnp.where(mask32, swap(fold), 0.0)], axis=0
        )
        flip = jnp.concatenate([p01, p2], axis=0).T
        u, w = flip[0:SIDE], flip[SIDE:128]
        k3[k, :, 0:128] = p01.astype(BF16)
        k3[k, :, 128:256] = p2.astype(BF16)
        kt3[k, :, 0:128] = jnp.where(mask, u, swap(w)).astype(BF16)
        kt3[k, :, 128:256] = jnp.where(mask, swap(u), 0.0).astype(BF16)
        zero = jnp.zeros((SIDE, 128), BF16)
        p01s = swap(p01)
        kst_lo[k, 0:64, :] = jnp.where(mask, p01, 0.0).astype(BF16)
        kst_lo[k, 64:128, :] = jnp.where(mask, p01s, 0.0).astype(BF16)
        kst_lo[k, 128:192, :] = p2.astype(BF16)
        kst_lo[k, 192:256, :] = zero
        kst_hi[k, 0:64, :] = jnp.where(mask, 0.0, p01s).astype(BF16)
        kst_hi[k, 64:128, :] = jnp.where(mask, 0.0, p01).astype(BF16)
        kst_hi[k, 128:192, :] = swap(p2).astype(BF16)
        kst_hi[k, 192:256, :] = zero

    def one_iteration(it, smem):
        home_weights(it)

        for half in range(2):
            def sum_body(j, carry, half=half):
                cols = pl.ds(pl.multiple_of(j * 128, 128), 128)
                x = dot(home_amp[...], mq[it, half, :, cols])
                to_stamps([x[0:16], x[16:32], x[32:48]], s_lo, s_hi, half * 16 + j)
                return carry

            lax.fori_loop(0, 16, sum_body, 0)

        def home_model(q, carry):
            if it == 0:
                @pl.when(jnp.logical_and(q != r, q < nk))
                def _():
                    pltpu.make_async_remote_copy(
                        src_ref=psf, dst_ref=kp.at[q], send_sem=psf_send.at[0],
                        recv_sem=psf_recv.at[q], device_id=sibling, device_id_type=MESH,
                    ).wait_recv()

                unpack(q)
            rows = pl.ds(pl.multiple_of(q * SIDE, SIDE), SIDE)
            s = jnp.concatenate([s_lo[rows, :], s_hi[rows, :]], axis=1).astype(BF16)
            kt = kt3[q]
            z = dot(s, block_diag(kt[:, 0:128], kt[:, 128:256])).astype(BF16)
            model[q] = dot(k3[q], block_diag(z[:, 0:128], z[:, 128:256]))
            return carry

        lax.fori_loop(0, SLOTS, home_model, 0)

        for d in range(4):
            amp_copy(it, d).wait_recv()
            picked = entries[pl.ds(CAP * d, CAP), :].astype(F32)
            cols = [
                jnp.sum(picked * amps_in[it, d, band : band + 1, :], axis=1, keepdims=True)
                for band in range(3)
            ]
            mask = lane_lo(CAP)
            rows = pl.ds(CAP * d, CAP)
            arep[rows, 0:128] = jnp.where(mask, cols[0], cols[1])
            arep[rows, 128:256] = jnp.where(mask, cols[2], 0.0)

        for d in range(4):
            vis_copy(it, d).wait_recv()
            fwd_copy(it, d, b).start()
        for d in range(4):
            fwd_copy(it, d, other).wait_recv()
        for half in range(2):
            def stamp_body(j, carry, half=half):
                cols = pl.ds(pl.multiple_of(j * 128, 128), 128)
                mask = lane_lo(64)
                xa = vin[it, half, 0:64, cols].astype(F32)
                xb = vin[it, half, 64:128, cols].astype(F32)
                pair = half * 16 + j
                xs[pl.ds(2 * pair, 64, stride=SIDE), :] = jnp.where(mask, xa, swap(xb))
                xs[pl.ds(2 * pair + 1, 64, stride=SIDE), :] = jnp.where(mask, swap(xa), xb)
                return carry

            lax.fori_loop(0, 16, stamp_body, 0)

        unroll = 4

        def visit_model(step, carry):
            acc = list(carry)
            blank = jnp.zeros((SIDE, 256), BF16)
            for u in range(unroll):
                p = step * unroll + u
                x = xs[pl.ds(pl.multiple_of(p * SIDE, SIDE), SIDE), :].astype(BF16)
                for side in range(2):
                    v = p + 64 * side
                    k = smem[0, v]
                    kt = kt3[k]
                    weights = jnp.concatenate([kt, blank] if side == 0 else [blank, kt], axis=0)
                    z = dot(x, weights).astype(BF16)
                    zs[v] = z
                    conv = dot(k3[k], block_diag(z[:, 0:128], z[:, 128:256]))
                    acc[side] = acc[side] + conv * arep[pl.ds(v, 1), :]
                    pfx[65 * side + p + 1] = acc[side]
            return tuple(acc)

        start = jnp.zeros((SIDE, 256), F32)
        lax.fori_loop(0, 64 // unroll, visit_model, (start, start))

        def home_back_body(q, carry):
            total = model[q]
            for d in range(4):
                base = (0, 32, 65, 97)[d]
                total = total + (pfx[base + smem[d + 2, q + 1]] - pfx[base + smem[d + 2, q]])
            rows = pl.ds(pl.multiple_of(q * SIDE, SIDE), SIDE)
            seen = jnp.concatenate([o_lo[rows, :], o_hi[rows, :]], axis=1)
            res = (total - seen).astype(BF16)
            diag = block_diag(res[:, 0:128], res[:, 128:256])
            resid[q] = diag
            t = dot(kt3[q], diag).astype(BF16)
            kk = k3[q]
            back = dot(t, block_diag(kk[:, 0:128], kk[:, 128:256]))
            b_lo[rows, :] = back[:, 0:128]
            b_hi[rows, :] = back[:, 128:256]
            return carry

        lax.fori_loop(0, SLOTS, home_back_body, 0)

        for half in range(2):
            def flat_body(j, carry, half=half):
                pair = half * 16 + j
                mask = lane_lo(SLOTS)
                even = pl.ds(2 * pair, SLOTS, stride=SIDE)
                odd = pl.ds(2 * pair + 1, SLOTS, stride=SIDE)
                e0, o0, e2, o2 = b_lo[even, :], b_lo[odd, :], b_hi[even, :], b_hi[odd, :]
                x = jnp.concatenate(
                    [
                        jnp.where(mask, e0, swap(o0)),
                        jnp.where(mask, swap(e0), o0),
                        jnp.where(mask, e2, swap(o2)),
                    ],
                    axis=0,
                )
                bflat[half, 0:48, pl.ds(pl.multiple_of(j * 128, 128), 128)] = x.astype(BF16)
                return carry

            lax.fori_loop(0, 16, flat_body, 0)

        def home_grad(j, carry):
            cols = pl.ds(pl.multiple_of(j * 256, 256), 256)
            hsend[it, :, cols] = dot(home_back[...], bflat[other, :, cols]).astype(BF16)
            hown[:, cols] = dot(home_back[...], bflat[b, :, cols])
            return carry

        lax.fori_loop(0, HALF // 256, home_grad, 0)
        home_copy(it).start()

        def home_gain(j, carry):
            cols = pl.ds(pl.multiple_of(j * 256, 256), 256)
            for half in range(2):
                carry = carry + lax.dot_general(
                    bflat[half, 0:48, cols], mq[it, half, :, cols], (((1,), (1,)), ((), ())),
                    preferred_element_type=F32,
                )
            return carry

        gain = lax.fori_loop(0, HALF // 256, home_gain, jnp.zeros((48, SRC), F32))
        ga_home[...] = jnp.concatenate(
            [
                jnp.sum(is_slot * gain[16 * band : 16 * band + 16], axis=0, keepdims=True)
                for band in range(3)
            ]
            + [jnp.zeros((5, SRC), F32)],
            axis=0,
        )

        def visit_back(step, carry):
            for u in range(unroll):
                p = step * unroll + u
                scaled, weights = [], []
                for side in range(2):
                    v = p + 64 * side
                    k = smem[0, v]
                    t = dot(kt3[k], resid[smem[1, v]])
                    ga_rows[pl.ds(v, 1), :] = jnp.sum(t * zs[v].astype(F32), axis=0, keepdims=True)
                    scaled.append((t * arep[pl.ds(v, 1), :]).astype(BF16))
                    weights.append(kst_lo[k] if side == 0 else kst_hi[k])
                gs[pl.ds(pl.multiple_of(p * SIDE, SIDE), SIDE), :] = dot(
                    scaled[0], weights[0]
                ) + dot(scaled[1], weights[1])
            return carry

        lax.fori_loop(0, 64 // unroll, visit_back, 0)

        for half in range(2):
            def grad_body(j, carry, half=half):
                pair = half * 16 + j
                mask = lane_lo(64)
                e = gs[pl.ds(2 * pair, 64, stride=SIDE), :]
                o = gs[pl.ds(2 * pair + 1, 64, stride=SIDE), :]
                cols = pl.ds(pl.multiple_of(j * 128, 128), 128)
                gflat[it, half, 0:64, cols] = jnp.where(mask, e, swap(o)).astype(BF16)
                gflat[it, half, 64:128, cols] = jnp.where(mask, swap(e), o).astype(BF16)
                return carry

            lax.fori_loop(0, 16, grad_body, 0)
        for d in range(4):
            part_copy(it, d, other).start()
        select = jnp.where(
            lax.broadcasted_iota(I32, (8, 256), 1) // SIDE
            == lax.broadcasted_iota(I32, (8, 256), 0),
            1.0,
            0.0,
        )
        ga_send[it] = lax.dot_general(
            select, ga_rows[...], (((1,), (1,)), ((), ())),
            preferred_element_type=F32, precision=lax.Precision.HIGHEST,
        )
        for d in range(4):
            gain_copy(it, d).start()
        for d in range(4):
            part_copy(it, d, other).wait_recv()
            rows = pl.ds(CAP * d, CAP)
            gsum[it, rows, :] = (
                gflat[it, b, rows, :].astype(F32) + gin[it, rows, :].astype(F32)
            ).astype(BF16)
            back_copy(it, d).start()

        lane = lax.broadcasted_iota(I32, (8, SRC), 1) // CAP
        returned = jnp.zeros((8, SRC), F32)
        for d in range(4):
            gain_copy(it, d).wait_recv()
            returned = returned + jnp.where(lane == d, ga_ret[it, d], 0.0)
        gain = ga_home[...] + jnp.dot(
            returned, pick_out[...], preferred_element_type=F32, precision=lax.Precision.HIGHEST
        )
        amp_now[...] = jnp.maximum(amp_now[...] - sstep[...] * gain, 0.0)
        if it == 0:
            amps[1] = amp_now[...].astype(BF16).astype(F32)
            for d in range(4):
                amp_copy(1, d).start()
        else:
            out_a[...] = amp_now[0:3, :]
        home_copy(it).wait_recv()
        for d in range(4):
            back_copy(it, d).wait_recv()

        def update(j, carry):
            cols = pl.ds(pl.multiple_of(j * 128, 128), 128)
            grad = hown[:, cols] + hin[it, :, cols].astype(F32)
            grad = grad + dot(pick_back[...], gret[it, :, cols])
            fresh = jnp.maximum(mf[:, cols] - step_col[...] * grad, 0.0)
            if it == 0:
                mf[:, cols] = fresh
                mq[1, b, :, cols] = fresh.astype(BF16)
            else:
                out_m[:, cols] = fresh
            return carry

        lax.fori_loop(0, HALF // 128, update, 0)
        if it == 0:
            send_visitors(1)
            mine_copy(b).start()
            mine_copy(other).wait_recv()

    pl.run_scoped(with_table, pltpu.SMEM((8, SRC), I32))

    for copy in list_copies:
        copy.wait_send()
    mine_copy(b).wait_send()
    for it in range(ITERS):
        home_copy(it).wait_send()
        for d in range(4):
            amp_copy(it, d).wait_send()
            vis_copy(it, d).wait_send()
            fwd_copy(it, d, b).wait_send()
            part_copy(it, d, other).wait_send()
            back_copy(it, d).wait_send()
            gain_copy(it, d).wait_send()

    @pl.when(r < SLOTS)
    def _():
        def body(step, carry):
            psf_copy(step).wait_send()
            return carry

        lax.fori_loop(1, n_ra, body, 0)


def shards(morphology, sed_amps, slot_lists, morph_step, sed_step, psf_kernels, observed):
    n_ra, n_dec = lax.axis_size("ra"), lax.axis_size("dec")
    kernels = psf_kernels.reshape(3, SIDE, SIDE)
    packed = jnp.concatenate(
        [
            jnp.concatenate([kernels[0], kernels[1]], axis=1),
            jnp.concatenate([kernels[2, :32], kernels[2, 32:]], axis=1),
        ],
        axis=0,
    )
    vmem = pl.BlockSpec(memory_space=pltpu.VMEM)
    dma = pltpu.SemaphoreType.DMA
    scratch = [
        pltpu.VMEM((SLOTS, 96, 128), BF16),
        pltpu.VMEM((SLOTS, SIDE, 256), BF16),
        pltpu.VMEM((SLOTS, SIDE, 256), BF16),
        pltpu.VMEM((SLOTS, 256, 128), BF16),
        pltpu.VMEM((SLOTS, 256, 128), BF16),
        pltpu.VMEM((8, SRC), I32),
        pltpu.VMEM((4, 8, SRC), I32),
        pltpu.VMEM((2, 8, SRC), F32),
        pltpu.VMEM((2, 4, 8, SRC), F32),
        pltpu.VMEM((8, SRC), F32),
        pltpu.VMEM((SRC, SRC), F32),
        pltpu.VMEM((SRC, SRC), BF16),
        pltpu.VMEM((48, SRC), BF16),
        pltpu.VMEM((SRC, SRC), BF16),
        pltpu.VMEM((SRC, SRC), F32),
        pltpu.VMEM((SRC, SRC), I32),
        pltpu.VMEM((8, SRC), I32),
        pltpu.VMEM((2, 2, SRC, HALF), BF16),
        pltpu.VMEM((SRC, HALF), F32),
        pltpu.VMEM((2, SRC, HALF), BF16),
        pltpu.VMEM((2, 2, SRC, HALF), BF16),
        pltpu.VMEM((64 * SIDE, 128), F32),
        pltpu.VMEM((SLOTS * SIDE, 128), F32),
        pltpu.VMEM((SLOTS * SIDE, 128), F32),
        pltpu.VMEM((SLOTS * SIDE, 128), F32),
        pltpu.VMEM((SLOTS * SIDE, 128), F32),
        pltpu.VMEM((SRC, SIDE, 256), BF16),
        pltpu.VMEM((130, SIDE, 256), F32),
        pltpu.VMEM((SLOTS, SIDE, 256), F32),
        pltpu.VMEM((SLOTS, 256, 256), BF16),
        pltpu.VMEM((SLOTS * SIDE, 128), F32),
        pltpu.VMEM((SLOTS * SIDE, 128), F32),
        pltpu.VMEM((2, SRC, HALF), BF16),
        pltpu.VMEM((64 * SIDE, 128), F32),
        pltpu.VMEM((2, 2, SRC, HALF), BF16),
        pltpu.VMEM((2, SRC, HALF), BF16),
        pltpu.VMEM((2, SRC, HALF), BF16),
        pltpu.VMEM((2, SRC, HALF), BF16),
        pltpu.VMEM((SRC, HALF), F32),
        pltpu.VMEM((2, SRC, HALF), BF16),
        pltpu.VMEM((2, SRC, HALF), BF16),
        pltpu.VMEM((SRC, 256), F32),
        pltpu.VMEM((SRC, 256), F32),
        pltpu.VMEM((2, 8, SRC), F32),
        pltpu.VMEM((2, 4, 8, SRC), F32),
        pltpu.VMEM((8, SRC), F32),
        dma((n_ra,)), dma((SLOTS,)),
        dma((2, 4)), dma((2, 2, 4)), dma((2, 2, 4)), dma((2, 2, 4)), dma((2, 1)), dma((2, 2)),
        dma((2, 2, 4)), dma((2, 2, 4)), dma((2, 2, 4)), dma,
    ]
    out_m, out_a = pl.pallas_call(
        functools.partial(deblend, n_ra, n_dec),
        out_shape=(
            jax.ShapeDtypeStruct((SRC, HALF), F32),
            jax.ShapeDtypeStruct((3, SRC), F32),
        ),
        in_specs=[vmem] * 7,
        out_specs=(vmem, vmem),
        scratch_shapes=scratch,
        compiler_params=pltpu.CompilerParams(
            collective_id=0, has_side_effects=True, vmem_limit_bytes=60 * 1024 * 1024
        ),
        name="deblend",
    )(
        morphology[0, 0], sed_amps[0, 0], slot_lists[0, 0], morph_step[0], sed_step[0],
        packed, observed[0, 0],
    )
    return out_m[None, None], out_a[None, None]


def solution(mesh):
    in_specs = (
        P("ra", "dec", None, None),
        P("ra", "dec", "band", None),
        P("ra", "dec", None, None),
        P("ra", "dec", None),
        P("ra", "dec", None),
        P("band", "ra", None),
        P("ra", "dec", "band", None, None),
    )
    out_specs = (P("ra", "dec", None, "band"), P("ra", "dec", "band", None))
    return jax.shard_map(shards, mesh=mesh, in_specs=in_specs, out_specs=out_specs, check_vma=False)
```

```python
import functools
import jax
import jax.numpy as jnp
from jax import lax
from jax.experimental import pallas as pl
from jax.experimental.pallas import tpu as pltpu
from jax.sharding import PartitionSpec as P

SIDE = 64
KERN = 32
ITERS = 2
SLOTS = 16
CAP = 32
SRC = 128
HALF = 2048
PITCH = 72
ROWS = 8
HOME = 8
PAIRS = 8
MESH = pl.DeviceIdType.MESH
F32 = jnp.float32
BF16 = jnp.bfloat16
I32 = jnp.int32


def lane_lo(rows):
    return lax.broadcasted_iota(I32, (rows, 128), 1) < SIDE


def swap(value):
    return pltpu.roll(value, SIDE, axis=1)


def block_diag(first, second):
    low = jnp.where(lane_lo(SIDE), 1.0, 0.0).astype(BF16)
    high = jnp.where(lane_lo(SIDE), 0.0, 1.0).astype(BF16)
    zero = jnp.zeros((SIDE, 128), BF16)
    return jnp.concatenate(
        [
            jnp.concatenate([first * low, zero], axis=1),
            jnp.concatenate([first * high, zero], axis=1),
            jnp.concatenate([zero, second], axis=1),
            jnp.concatenate([zero, zero], axis=1),
        ],
        axis=0,
    )


def dot(a, b):
    return jnp.dot(a, b, preferred_element_type=F32)


def tiled(count, unroll, body):
    def steps(step, carry):
        for u in range(unroll):
            body(step * unroll + u, carry)
        return carry

    lax.fori_loop(0, count // unroll, steps, 0)


def turned(row):
    return jnp.broadcast_to(row, (SRC, SRC)).T


def places(row):
    source = lax.broadcasted_iota(I32, (1, SRC), 1)
    key_row = row * SRC + source
    column = turned(row)
    key_col = column * SRC + lax.broadcasted_iota(I32, (SRC, SRC), 0)
    rank = jnp.sum(jnp.where(key_col < key_row, 1, 0), axis=0, keepdims=True)
    below = jnp.sum(
        jnp.where(column < lax.broadcasted_iota(I32, (SRC, SRC), 1), 1, 0), axis=0, keepdims=True
    )
    return rank, below


def chosen(row, rank):
    entry = lax.broadcasted_iota(I32, (CAP, SRC), 0)
    return jnp.where(rank == entry, 1, 0) * jnp.where(row < SLOTS, 1, 0)


def to_stamps(parts, low_ref, high_ref, pair):
    x0, x1, x2 = parts
    mask = lane_lo(SLOTS)
    even, odd = pl.ds(2 * pair, SLOTS, stride=PITCH), pl.ds(2 * pair + 1, SLOTS, stride=PITCH)
    low_ref[even, :] = jnp.where(mask, x0, swap(x1))
    low_ref[odd, :] = jnp.where(mask, swap(x0), x1)
    high_ref[even, :] = jnp.where(mask, x2, 0.0)
    high_ref[odd, :] = jnp.where(mask, swap(x2), 0.0)


def deblend(
    n_ra, n_dec,
    morph, sed, lists, mstep, sstep, psf, obs,
    out_m, out_a,
    kp, k3, kt3, kst_lo, kst_hi,
    lists8, lists_in, amps, amps_in, amp_now,
    pick_out, pick_back, home_amp, home_back, step_col, entries, table,
    mq, mf, vout, vin, xs, s_lo, s_hi, o_lo, o_hi, zs, pfx, model, resid,
    b_lo, b_hi, bflat, gs, gflat, gsum, gin, gret, hown, hsend, hin,
    arep, ga_rows, ga_send, ga_ret, ga_home,
    psf_send, psf_recv, list_sem, amp_sem, vis_sem, fwd_sem, mine_sem, home_sem,
    part_sem, back_sem, gain_sem, table_sem,
):
    r = lax.axis_index("ra")
    c = lax.axis_index("dec")
    b = lax.axis_index("band")
    other = 1 - b
    right, left = lax.rem(r + 1, n_ra), lax.rem(r + n_ra - 1, n_ra)
    up, down = lax.rem(c + 1, n_dec), lax.rem(c + n_dec - 1, n_dec)
    target = [(right, c, b), (left, c, b), (r, up, b), (r, down, b)]
    origin = [(left, c, b), (right, c, b), (r, down, b), (r, up, b)]
    sibling = (r, c, other)
    nk = min(SLOTS, n_ra)

    def send(src, dst, sems, index, device):
        return pltpu.make_async_remote_copy(
            src_ref=src, dst_ref=dst,
            send_sem=sems.at[(0,) + index], recv_sem=sems.at[(1,) + index],
            device_id=device, device_id_type=MESH,
        )

    barrier = pltpu.get_barrier_semaphore()

    def greet(step, carry):
        pl.semaphore_signal(
            barrier, inc=1, device_id=(lax.rem(r + step, n_ra), c, b), device_id_type=MESH
        )
        return carry

    lax.fori_loop(1, n_ra, greet, 0)
    for device in target[2:] + [sibling]:
        pl.semaphore_signal(barrier, inc=1, device_id=device, device_id_type=MESH)
    lists8[...] = jnp.full((8, SRC), SLOTS, I32)
    lists8[0:5, :] = lists[...]
    amp_now[...] = jnp.zeros((8, SRC), F32)
    amp_now[0:3, :] = sed[...]
    amps[0] = amp_now[...].astype(BF16).astype(F32)
    pl.semaphore_wait(barrier, n_ra - 1 + 3)

    list_copies = [
        send(lists8, lists_in.at[d], list_sem, (d,), target[d]) for d in range(4)
    ]
    for copy in list_copies:
        copy.start()

    def psf_copy(step):
        return pltpu.make_async_remote_copy(
            src_ref=psf, dst_ref=kp.at[lax.rem(r, SLOTS)],
            send_sem=psf_send.at[step], recv_sem=psf_recv.at[lax.rem(r, SLOTS)],
            device_id=(lax.rem(r + step, n_ra), c, b), device_id_type=MESH,
        )

    def spread_psf():
        def body(step, carry):
            psf_copy(step).start()
            return carry

        lax.fori_loop(1, n_ra, body, 0)
        kp[lax.rem(r, SLOTS)] = psf[...]

    def amp_copy(it, d):
        return send(amps.at[it], amps_in.at[it, d], amp_sem, (it, d), target[d])

    def vis_copy(it, d):
        rows = pl.ds(CAP * d, CAP)
        return send(vout.at[it, rows], vin.at[it, b, rows], vis_sem, (it, d), target[d])

    def fwd_copy(it, d, half):
        rows = pl.ds(CAP * d, CAP)
        return send(vin.at[it, half, rows], vin.at[it, half, rows], fwd_sem, (it, d), sibling)

    def mine_copy(half):
        return send(mq.at[1, half], mq.at[1, half], mine_sem, (0,), sibling)

    def home_copy(it):
        return send(hsend.at[it], hin.at[it], home_sem, (it,), sibling)

    def part_copy(it, d, half):
        rows = pl.ds(CAP * d, CAP)
        return send(gflat.at[it, half, rows], gin.at[it, rows], part_sem, (it, d), sibling)

    def back_copy(it, d):
        rows = pl.ds(CAP * d, CAP)
        return send(gsum.at[it, rows], gret.at[it, rows], back_sem, (it, d), origin[d])

    def gain_copy(it, d):
        return send(ga_send.at[it], ga_ret.at[it, d], gain_sem, (it, d), origin[d])

    for d in range(4):
        amp_copy(0, d).start()

    for d in range(4):
        row = lists8[d + 1 : d + 2, :]
        rank, _ = places(row)
        entries[pl.ds(CAP * d, CAP), :] = chosen(row, rank)
    pick = entries[...].astype(F32)
    pick_out[...] = pick
    pick_back[...] = pick.T.astype(BF16)

    mq[0, 0] = morph[:, 0:HALF]
    mq[0, 1] = morph[:, HALF : 2 * HALF]
    mf[...] = mq[0, b].astype(F32)

    def send_visitors(it):
        def body(j, carry):
            cols = pl.ds(pl.multiple_of(j * 256, 256), 256)
            vout[it, :, cols] = dot(pick_out[...].astype(BF16), mq[it, b, :, cols]).astype(BF16)
            return carry

        lax.fori_loop(0, HALF // 256, body, 0)
        for d in range(4):
            vis_copy(it, d).start()

    send_visitors(0)

    @pl.when(r < SLOTS)
    def _():
        spread_psf()

    if nk < SLOTS:
        kp[nk:SLOTS] = jnp.zeros((SLOTS - nk, 96, 128), BF16)

    step_col[...] = turned(mstep[...])
    slot0 = lists8[0:1, :]
    is_slot = jnp.where(slot0 == lax.broadcasted_iota(I32, (SLOTS, SRC), 0), 1.0, 0.0)
    bflat[...] = jnp.zeros(bflat.shape, BF16)
    pfx[0] = jnp.zeros((SIDE, 256), F32)
    pfx[65] = jnp.zeros((SIDE, 256), F32)

    for half in range(2):
        def obs_body(j, carry, half=half):
            cols = pl.ds(pl.multiple_of((half * 16 + j) * 128, 128), 128)
            parts = [obs[band, :, cols].astype(F32) for band in range(3)]
            to_stamps(parts, o_lo, o_hi, half * 16 + j)
            return carry

        tiled(16, ROWS, obs_body)

    def take_lists():
        table[...] = jnp.zeros((8, SRC), I32)
        for d in range(4):
            list_copies[d].wait_recv()
            row = lists_in[d, d + 1 : d + 2, :]
            rank, below = places(row)
            picked = chosen(row, rank)
            entries[pl.ds(CAP * d, CAP), :] = picked
            table[d + 2 : d + 3, :] = jnp.minimum(below, CAP)
        first, second = [], []
        for d in range(4):
            picked = entries[pl.ds(CAP * d, CAP), :]
            first.append(picked * lists_in[d, 0:1, :])
            second.append(picked * lists_in[d, d + 1 : d + 2, :])
        table[0:1, :] = jnp.minimum(
            jnp.sum(jnp.concatenate(first, axis=0).T, axis=0, keepdims=True), SLOTS - 1
        )
        table[1:2, :] = jnp.minimum(
            jnp.sum(jnp.concatenate(second, axis=0).T, axis=0, keepdims=True), SLOTS - 1
        )

    take_lists()

    def with_table(smem):
        copy = pltpu.make_async_copy(table, smem, table_sem)
        copy.start()
        copy.wait()
        for it in range(ITERS):
            one_iteration(it, smem)

    def home_weights(it):
        rows = [is_slot * amps[it, band : band + 1, :] for band in range(3)]
        full = jnp.concatenate(rows + [jnp.zeros((SRC - 48, SRC), F32)], axis=0)
        home_amp[...] = full[0:48].astype(BF16)
        home_back[...] = full.T.astype(BF16)

    def unpack(k):
        mask = lane_lo(SIDE)
        p01 = kp[k, 0:SIDE, :].astype(F32)
        fold = kp[k, SIDE:96, :].astype(F32)
        mask32 = lane_lo(32)
        p2 = jnp.concatenate(
            [jnp.where(mask32, fold, 0.0), jnp.where(mask32, swap(fold), 0.0)], axis=0
        )
        flip = jnp.concatenate([p01, p2], axis=0).T
        u, w = flip[0:SIDE], flip[SIDE:128]
        k3[k, :, 0:128] = p01.astype(BF16)
        k3[k, :, 128:256] = p2.astype(BF16)
        kt3[k, :, 0:128] = jnp.where(mask, u, swap(w)).astype(BF16)
        kt3[k, :, 128:256] = jnp.where(mask, swap(u), 0.0).astype(BF16)
        zero = jnp.zeros((SIDE, 128), BF16)
        p01s = swap(p01)
        kst_lo[k, 0:64, :] = jnp.where(mask, p01, 0.0).astype(BF16)
        kst_lo[k, 64:128, :] = jnp.where(mask, p01s, 0.0).astype(BF16)
        kst_lo[k, 128:192, :] = p2.astype(BF16)
        kst_lo[k, 192:256, :] = zero
        kst_hi[k, 0:64, :] = jnp.where(mask, 0.0, p01s).astype(BF16)
        kst_hi[k, 64:128, :] = jnp.where(mask, 0.0, p01).astype(BF16)
        kst_hi[k, 128:192, :] = swap(p2).astype(BF16)
        kst_hi[k, 192:256, :] = zero

    def one_iteration(it, smem):
        home_weights(it)

        for half in range(2):
            def sum_body(j, carry, half=half):
                cols = pl.ds(pl.multiple_of(j * 128, 128), 128)
                x = dot(home_amp[...], mq[it, half, :, cols])
                to_stamps([x[0:16], x[16:32], x[32:48]], s_lo, s_hi, half * 16 + j)
                return carry

            tiled(16, ROWS, sum_body)

        if it == 0:
            def ready(q, carry):
                @pl.when(jnp.logical_and(q != r, q < nk))
                def _():
                    pltpu.make_async_remote_copy(
                        src_ref=psf, dst_ref=kp.at[q], send_sem=psf_send.at[0],
                        recv_sem=psf_recv.at[q], device_id=sibling, device_id_type=MESH,
                    ).wait_recv()

                return carry

            lax.fori_loop(0, SLOTS, ready, 0)

            def unpack_body(q, carry):
                unpack(q)
                return carry

            tiled(SLOTS, 4, unpack_body)

        def home_model(step, carry):
            slots = [step * HOME + u for u in range(HOME)]
            z = []
            for q in slots:
                rows = pl.ds(pl.multiple_of(q * PITCH, 8), SIDE)
                s = jnp.concatenate([s_lo[rows, :], s_hi[rows, :]], axis=1).astype(BF16)
                kt = kt3[q]
                z.append(dot(s, block_diag(kt[:, 0:128], kt[:, 128:256])).astype(BF16))
            for q, zq in zip(slots, z):
                model[q] = dot(k3[q], block_diag(zq[:, 0:128], zq[:, 128:256]))
            return carry

        lax.fori_loop(0, SLOTS // HOME, home_model, 0)

        for d in range(4):
            amp_copy(it, d).wait_recv()
            picked = entries[pl.ds(CAP * d, CAP), :].astype(F32)
            cols = [
                jnp.sum(picked * amps_in[it, d, band : band + 1, :], axis=1, keepdims=True)
                for band in range(3)
            ]
            mask = lane_lo(CAP)
            rows = pl.ds(CAP * d, CAP)
            arep[rows, 0:128] = jnp.where(mask, cols[0], cols[1])
            arep[rows, 128:256] = jnp.where(mask, cols[2], 0.0)

        for d in range(4):
            vis_copy(it, d).wait_recv()
            fwd_copy(it, d, b).start()
        for d in range(4):
            fwd_copy(it, d, other).wait_recv()
        for half in range(2):
            def stamp_body(j, carry, half=half):
                cols = pl.ds(pl.multiple_of(j * 128, 128), 128)
                mask = lane_lo(64)
                xa = vin[it, half, 0:64, cols].astype(F32)
                xb = vin[it, half, 64:128, cols].astype(F32)
                pair = half * 16 + j
                xs[pl.ds(2 * pair, 64, stride=PITCH), :] = jnp.where(mask, xa, swap(xb))
                xs[pl.ds(2 * pair + 1, 64, stride=PITCH), :] = jnp.where(mask, swap(xa), xb)
                return carry

            tiled(16, ROWS, stamp_body)

        def visit_model(step, carry):
            acc = list(carry)
            blank = jnp.zeros((SIDE, 256), BF16)
            pairs = [step * PAIRS + u for u in range(PAIRS)]
            which = [[smem[0, p + 64 * side] for side in range(2)] for p in pairs]
            z = []
            for p, ks in zip(pairs, which):
                x = xs[pl.ds(pl.multiple_of(p * PITCH, 8), SIDE), :].astype(BF16)
                for side in range(2):
                    kt = kt3[ks[side]]
                    weights = jnp.concatenate([kt, blank] if side == 0 else [blank, kt], axis=0)
                    z.append(dot(x, weights).astype(BF16))
            for u, (p, ks) in enumerate(zip(pairs, which)):
                for side in range(2):
                    v = p + 64 * side
                    zv = z[2 * u + side]
                    zs[v] = zv
                    conv = dot(k3[ks[side]], block_diag(zv[:, 0:128], zv[:, 128:256]))
                    acc[side] = acc[side] + conv * arep[pl.ds(v, 1), :]
                    pfx[65 * side + p + 1] = acc[side]
            return tuple(acc)

        start = jnp.zeros((SIDE, 256), F32)
        lax.fori_loop(0, 64 // PAIRS, visit_model, (start, start))

        def home_back_body(step, carry):
            slots = [step * HOME + u for u in range(HOME)]
            diags = []
            for q in slots:
                total = model[q]
                for d in range(4):
                    base = (0, 32, 65, 97)[d]
                    total = total + (pfx[base + smem[d + 2, q + 1]] - pfx[base + smem[d + 2, q]])
                rows = pl.ds(pl.multiple_of(q * PITCH, 8), SIDE)
                seen = jnp.concatenate([o_lo[rows, :], o_hi[rows, :]], axis=1)
                res = (total - seen).astype(BF16)
                diags.append(block_diag(res[:, 0:128], res[:, 128:256]))
                resid[q] = diags[-1]
            turns = [dot(kt3[q], diag).astype(BF16) for q, diag in zip(slots, diags)]
            for q, t in zip(slots, turns):
                rows = pl.ds(pl.multiple_of(q * PITCH, 8), SIDE)
                kk = k3[q]
                back = dot(t, block_diag(kk[:, 0:128], kk[:, 128:256]))
                b_lo[rows, :] = back[:, 0:128]
                b_hi[rows, :] = back[:, 128:256]
            return carry

        lax.fori_loop(0, SLOTS // HOME, home_back_body, 0)

        for half in range(2):
            def flat_body(j, carry, half=half):
                pair = half * 16 + j
                mask = lane_lo(SLOTS)
                even = pl.ds(2 * pair, SLOTS, stride=PITCH)
                odd = pl.ds(2 * pair + 1, SLOTS, stride=PITCH)
                e0, o0, e2, o2 = b_lo[even, :], b_lo[odd, :], b_hi[even, :], b_hi[odd, :]
                x = jnp.concatenate(
                    [
                        jnp.where(mask, e0, swap(o0)),
                        jnp.where(mask, swap(e0), o0),
                        jnp.where(mask, e2, swap(o2)),
                    ],
                    axis=0,
                )
                bflat[half, 0:48, pl.ds(pl.multiple_of(j * 128, 128), 128)] = x.astype(BF16)
                return carry

            tiled(16, ROWS, flat_body)

        def home_grad(j, carry):
            cols = pl.ds(pl.multiple_of(j * 256, 256), 256)
            hsend[it, :, cols] = dot(home_back[...], bflat[other, :, cols]).astype(BF16)
            hown[:, cols] = dot(home_back[...], bflat[b, :, cols])
            return carry

        tiled(8, 4, home_grad)
        home_copy(it).start()

        def home_gain(j, carry):
            cols = pl.ds(pl.multiple_of(j * 256, 256), 256)
            for half in range(2):
                carry = carry + lax.dot_general(
                    bflat[half, 0:48, cols], mq[it, half, :, cols], (((1,), (1,)), ((), ())),
                    preferred_element_type=F32,
                )
            return carry

        gain = lax.fori_loop(0, HALF // 256, home_gain, jnp.zeros((48, SRC), F32))
        ga_home[...] = jnp.concatenate(
            [
                jnp.sum(is_slot * gain[16 * band : 16 * band + 16], axis=0, keepdims=True)
                for band in range(3)
            ]
            + [jnp.zeros((5, SRC), F32)],
            axis=0,
        )

        def visit_back(step, carry):
            pairs = [step * PAIRS + u for u in range(PAIRS)]
            which = [[smem[0, p + 64 * side] for side in range(2)] for p in pairs]
            scaled = []
            for p, ks in zip(pairs, which):
                for side in range(2):
                    v = p + 64 * side
                    t = dot(kt3[ks[side]], resid[smem[1, v]])
                    ga_rows[pl.ds(v, 1), :] = jnp.sum(t * zs[v].astype(F32), axis=0, keepdims=True)
                    scaled.append((t * arep[pl.ds(v, 1), :]).astype(BF16))
            for u, (p, ks) in enumerate(zip(pairs, which)):
                gs[pl.ds(pl.multiple_of(p * PITCH, 8), SIDE), :] = dot(
                    scaled[2 * u], kst_lo[ks[0]]
                ) + dot(scaled[2 * u + 1], kst_hi[ks[1]])
            return carry

        lax.fori_loop(0, 64 // PAIRS, visit_back, 0)

        for half in range(2):
            def grad_body(j, carry, half=half):
                pair = half * 16 + j
                mask = lane_lo(64)
                e = gs[pl.ds(2 * pair, 64, stride=PITCH), :]
                o = gs[pl.ds(2 * pair + 1, 64, stride=PITCH), :]
                cols = pl.ds(pl.multiple_of(j * 128, 128), 128)
                gflat[it, half, 0:64, cols] = jnp.where(mask, e, swap(o)).astype(BF16)
                gflat[it, half, 64:128, cols] = jnp.where(mask, swap(e), o).astype(BF16)
                return carry

            tiled(16, ROWS, grad_body)
        for d in range(4):
            part_copy(it, d, other).start()
        select = jnp.where(
            lax.broadcasted_iota(I32, (8, 256), 1) // SIDE
            == lax.broadcasted_iota(I32, (8, 256), 0),
            1.0,
            0.0,
        )
        ga_send[it] = lax.dot_general(
            select, ga_rows[...], (((1,), (1,)), ((), ())),
            preferred_element_type=F32, precision=lax.Precision.HIGHEST,
        )
        for d in range(4):
            gain_copy(it, d).start()
        for d in range(4):
            part_copy(it, d, other).wait_recv()
            rows = pl.ds(CAP * d, CAP)
            gsum[it, rows, :] = (
                gflat[it, b, rows, :].astype(F32) + gin[it, rows, :].astype(F32)
            ).astype(BF16)
            back_copy(it, d).start()

        lane = lax.broadcasted_iota(I32, (8, SRC), 1) // CAP
        returned = jnp.zeros((8, SRC), F32)
        for d in range(4):
            gain_copy(it, d).wait_recv()
            returned = returned + jnp.where(lane == d, ga_ret[it, d], 0.0)
        gain = ga_home[...] + jnp.dot(
            returned, pick_out[...], preferred_element_type=F32, precision=lax.Precision.HIGHEST
        )
        amp_now[...] = jnp.maximum(amp_now[...] - sstep[...] * gain, 0.0)
        if it == 0:
            amps[1] = amp_now[...].astype(BF16).astype(F32)
            for d in range(4):
                amp_copy(1, d).start()
        else:
            out_a[...] = amp_now[0:3, :]
        home_copy(it).wait_recv()
        for d in range(4):
            back_copy(it, d).wait_recv()

        def update(j, carry):
            cols = pl.ds(pl.multiple_of(j * 128, 128), 128)
            grad = hown[:, cols] + hin[it, :, cols].astype(F32)
            grad = grad + dot(pick_back[...], gret[it, :, cols])
            fresh = jnp.maximum(mf[:, cols] - step_col[...] * grad, 0.0)
            if it == 0:
                mf[:, cols] = fresh
                mq[1, b, :, cols] = fresh.astype(BF16)
            else:
                out_m[:, cols] = fresh
            return carry

        tiled(16, ROWS, update)
        if it == 0:
            send_visitors(1)
            mine_copy(b).start()
            mine_copy(other).wait_recv()

    pl.run_scoped(with_table, pltpu.SMEM((8, SRC), I32))

    for copy in list_copies:
        copy.wait_send()
    mine_copy(b).wait_send()
    for it in range(ITERS):
        home_copy(it).wait_send()
        for d in range(4):
            amp_copy(it, d).wait_send()
            vis_copy(it, d).wait_send()
            fwd_copy(it, d, b).wait_send()
            part_copy(it, d, other).wait_send()
            back_copy(it, d).wait_send()
            gain_copy(it, d).wait_send()

    @pl.when(r < SLOTS)
    def _():
        def body(step, carry):
            psf_copy(step).wait_send()
            return carry

        lax.fori_loop(1, n_ra, body, 0)


def shards(morphology, sed_amps, slot_lists, morph_step, sed_step, psf_kernels, observed):
    n_ra, n_dec = lax.axis_size("ra"), lax.axis_size("dec")
    kernels = psf_kernels.reshape(3, SIDE, SIDE)
    packed = jnp.concatenate(
        [
            jnp.concatenate([kernels[0], kernels[1]], axis=1),
            jnp.concatenate([kernels[2, :32], kernels[2, 32:]], axis=1),
        ],
        axis=0,
    )
    vmem = pl.BlockSpec(memory_space=pltpu.VMEM)
    dma = pltpu.SemaphoreType.DMA
    scratch = [
        pltpu.VMEM((SLOTS, 96, 128), BF16),
        pltpu.VMEM((SLOTS, SIDE, 256), BF16),
        pltpu.VMEM((SLOTS, SIDE, 256), BF16),
        pltpu.VMEM((SLOTS, 256, 128), BF16),
        pltpu.VMEM((SLOTS, 256, 128), BF16),
        pltpu.VMEM((8, SRC), I32),
        pltpu.VMEM((4, 8, SRC), I32),
        pltpu.VMEM((2, 8, SRC), F32),
        pltpu.VMEM((2, 4, 8, SRC), F32),
        pltpu.VMEM((8, SRC), F32),
        pltpu.VMEM((SRC, SRC), F32),
        pltpu.VMEM((SRC, SRC), BF16),
        pltpu.VMEM((48, SRC), BF16),
        pltpu.VMEM((SRC, SRC), BF16),
        pltpu.VMEM((SRC, SRC), F32),
        pltpu.VMEM((SRC, SRC), I32),
        pltpu.VMEM((8, SRC), I32),
        pltpu.VMEM((2, 2, SRC, HALF), BF16),
        pltpu.VMEM((SRC, HALF), F32),
        pltpu.VMEM((2, SRC, HALF), BF16),
        pltpu.VMEM((2, 2, SRC, HALF), BF16),
        pltpu.VMEM((64 * PITCH, 128), F32),
        pltpu.VMEM((SLOTS * PITCH, 128), F32),
        pltpu.VMEM((SLOTS * PITCH, 128), F32),
        pltpu.VMEM((SLOTS * PITCH, 128), F32),
        pltpu.VMEM((SLOTS * PITCH, 128), F32),
        pltpu.VMEM((SRC, SIDE, 256), BF16),
        pltpu.VMEM((130, SIDE, 256), F32),
        pltpu.VMEM((SLOTS, SIDE, 256), F32),
        pltpu.VMEM((SLOTS, 256, 256), BF16),
        pltpu.VMEM((SLOTS * PITCH, 128), F32),
        pltpu.VMEM((SLOTS * PITCH, 128), F32),
        pltpu.VMEM((2, SRC, HALF), BF16),
        pltpu.VMEM((64 * PITCH, 128), F32),
        pltpu.VMEM((2, 2, SRC, HALF), BF16),
        pltpu.VMEM((2, SRC, HALF), BF16),
        pltpu.VMEM((2, SRC, HALF), BF16),
        pltpu.VMEM((2, SRC, HALF), BF16),
        pltpu.VMEM((SRC, HALF), F32),
        pltpu.VMEM((2, SRC, HALF), BF16),
        pltpu.VMEM((2, SRC, HALF), BF16),
        pltpu.VMEM((SRC, 256), F32),
        pltpu.VMEM((SRC, 256), F32),
        pltpu.VMEM((2, 8, SRC), F32),
        pltpu.VMEM((2, 4, 8, SRC), F32),
        pltpu.VMEM((8, SRC), F32),
        dma((n_ra,)), dma((SLOTS,)),
        dma((2, 4)), dma((2, 2, 4)), dma((2, 2, 4)), dma((2, 2, 4)), dma((2, 1)), dma((2, 2)),
        dma((2, 2, 4)), dma((2, 2, 4)), dma((2, 2, 4)), dma,
    ]
    out_m, out_a = pl.pallas_call(
        functools.partial(deblend, n_ra, n_dec),
        out_shape=(
            jax.ShapeDtypeStruct((SRC, HALF), F32),
            jax.ShapeDtypeStruct((3, SRC), F32),
        ),
        in_specs=[vmem] * 7,
        out_specs=(vmem, vmem),
        scratch_shapes=scratch,
        compiler_params=pltpu.CompilerParams(
            collective_id=0, has_side_effects=True, vmem_limit_bytes=60 * 1024 * 1024
        ),
        name="deblend",
    )(
        morphology[0, 0], sed_amps[0, 0], slot_lists[0, 0], morph_step[0], sed_step[0],
        packed, observed[0, 0],
    )
    return out_m[None, None], out_a[None, None]


def solution(mesh):
    in_specs = (
        P("ra", "dec", None, None),
        P("ra", "dec", "band", None),
        P("ra", "dec", None, None),
        P("ra", "dec", None),
        P("ra", "dec", None),
        P("band", "ra", None),
        P("ra", "dec", "band", None, None),
    )
    out_specs = (P("ra", "dec", None, "band"), P("ra", "dec", "band", None))
    return jax.shard_map(shards, mesh=mesh, in_specs=in_specs, out_specs=out_specs, check_vma=False)
```

```python
import functools
import jax
import jax.numpy as jnp
from jax import lax
from jax.experimental import pallas as pl
from jax.experimental.pallas import tpu as pltpu
from jax.sharding import PartitionSpec as P

SIDE = 64
KERN = 32
ITERS = 2
SLOTS = 16
CAP = 32
SRC = 128
HALF = 2048
PITCH = 72
ROWS = 8
HOME = 8
PAIRS = 8
MESH = pl.DeviceIdType.MESH
F32 = jnp.float32
BF16 = jnp.bfloat16
I32 = jnp.int32


def lane_lo(rows):
    return lax.broadcasted_iota(I32, (rows, 128), 1) < SIDE


def swap(value):
    return pltpu.roll(value, SIDE, axis=1)


def block_diag(first, second):
    low = jnp.where(lane_lo(SIDE), 1.0, 0.0).astype(BF16)
    high = jnp.where(lane_lo(SIDE), 0.0, 1.0).astype(BF16)
    zero = jnp.zeros((SIDE, 128), BF16)
    return jnp.concatenate(
        [
            jnp.concatenate([first * low, zero], axis=1),
            jnp.concatenate([first * high, zero], axis=1),
            jnp.concatenate([zero, second], axis=1),
            jnp.concatenate([zero, zero], axis=1),
        ],
        axis=0,
    )


def dot(a, b):
    return jnp.dot(a, b, preferred_element_type=F32)


def tiled(count, unroll, body):
    def steps(step, carry):
        for u in range(unroll):
            body(step * unroll + u, carry)
        return carry

    lax.fori_loop(0, count // unroll, steps, 0)


def turned(row):
    return jnp.broadcast_to(row, (SRC, SRC)).T


def places(row):
    source = lax.broadcasted_iota(I32, (1, SRC), 1)
    key_row = row * SRC + source
    column = turned(row)
    key_col = column * SRC + lax.broadcasted_iota(I32, (SRC, SRC), 0)
    rank = jnp.sum(jnp.where(key_col < key_row, 1, 0), axis=0, keepdims=True)
    below = jnp.sum(
        jnp.where(column < lax.broadcasted_iota(I32, (SRC, SRC), 1), 1, 0), axis=0, keepdims=True
    )
    return rank, below


def chosen(row, rank):
    entry = lax.broadcasted_iota(I32, (CAP, SRC), 0)
    return jnp.where(rank == entry, 1, 0) * jnp.where(row < SLOTS, 1, 0)


def to_stamps(parts, low_ref, high_ref, pair):
    x0, x1, x2 = parts
    mask = lane_lo(SLOTS)
    even, odd = pl.ds(2 * pair, SLOTS, stride=PITCH), pl.ds(2 * pair + 1, SLOTS, stride=PITCH)
    low_ref[even, :] = jnp.where(mask, x0, swap(x1))
    low_ref[odd, :] = jnp.where(mask, swap(x0), x1)
    high_ref[even, :] = jnp.where(mask, x2, 0.0)
    high_ref[odd, :] = jnp.where(mask, swap(x2), 0.0)


def deblend(
    n_ra, n_dec, n_x,
    morph, sed, lists, mstep, sstep, psf_in, obs_in,
    out_m, out_a,
    psf_f, psf, obs, kp, k3, kt3, kst_lo, kst_hi,
    lists8, lists_in, amps, amps_in, amp_now,
    pick_out, pick_back, home_amp, home_back, step_col, entries, table,
    mq, mf, vout, vin, xs, s_lo, s_hi, o_lo, o_hi, zs, pfx, model, resid,
    b_lo, b_hi, bflat, gs, gflat, gsum, gin, gret, hown, hsend, hin,
    arep, ga_rows, ga_send, ga_ret, ga_home,
    psf_send, psf_recv, list_sem, amp_sem, vis_sem, fwd_sem, mine_sem, home_sem,
    part_sem, back_sem, gain_sem, table_sem, load_sem,
):
    r = lax.axis_index("ra")
    c = lax.axis_index("dec")
    b = lax.axis_index("band")
    other = 1 - b
    right, left = lax.rem(r + 1, n_ra), lax.rem(r + n_ra - 1, n_ra)
    up, down = lax.rem(c + 1, n_dec), lax.rem(c + n_dec - 1, n_dec)
    target = [(right, c, b), (left, c, b), (r, up, b), (r, down, b)]
    origin = [(left, c, b), (right, c, b), (r, down, b), (r, up, b)]
    sibling = (r, c, other)
    n_z = n_ra // n_x
    x, z = r // n_z, lax.rem(r, n_z)
    kind = lax.rem(c, 2)
    kind_k = kind * n_z
    partner = (r, c + 1 - 2 * kind, b)

    def send(src, dst, sems, index, device):
        return pltpu.make_async_remote_copy(
            src_ref=src, dst_ref=dst,
            send_sem=sems.at[(0,) + index], recv_sem=sems.at[(1,) + index],
            device_id=device, device_id_type=MESH,
        )

    def x_peer(step):
        return (lax.rem(x + step, n_x) * n_z + z, c, b)

    def z_peer(step):
        return (x * n_z + lax.rem(z + step, n_z), c, b)

    barrier = pltpu.get_barrier_semaphore()
    for device in (
        target
        + [sibling]
        + [x_peer(step) for step in range(1, n_x)]
        + [z_peer(step) for step in range(1, n_z)]
    ):
        pl.semaphore_signal(barrier, inc=1, device_id=device, device_id_type=MESH)
    loads = [
        pltpu.make_async_copy(morph.at[:, pl.ds(HALF * half, HALF)], mq.at[0, half], load_sem.at[half])
        for half in range(2)
    ] + [pltpu.make_async_copy(obs_in, obs, load_sem.at[2])]
    for load in loads:
        load.start()
    lists8[...] = jnp.full((8, SRC), SLOTS, I32)
    for d in range(5):
        lists8[d : d + 1, :] = lists[d]
    amp_now[...] = jnp.zeros((8, SRC), F32)
    for band in range(3):
        amp_now[band : band + 1, :] = sed[band]
    amps[0] = amp_now[...].astype(BF16).astype(F32)
    own = psf_in[...].astype(F32)
    for j in range(32):
        x0, x1 = own[0:1, 128 * j : 128 * j + 128], own[1:2, 128 * j : 128 * j + 128]
        psf_f[2 * j : 2 * j + 1, :] = jnp.where(lane_lo(1), x0, swap(x1))
        psf_f[2 * j + 1 : 2 * j + 2, :] = jnp.where(lane_lo(1), swap(x0), x1)
    for j in range(16):
        x0 = own[2:3, 128 * j : 128 * j + 128]
        x1 = own[2:3, HALF + 128 * j : HALF + 128 * j + 128]
        psf_f[64 + 2 * j : 65 + 2 * j, :] = jnp.where(lane_lo(1), x0, swap(x1))
        psf_f[65 + 2 * j : 66 + 2 * j, :] = jnp.where(lane_lo(1), swap(x0), x1)
    psf[...] = psf_f[...].astype(BF16)
    pl.semaphore_wait(barrier, 5 + n_x - 1 + n_z - 1)

    list_copies = [
        send(lists8, lists_in.at[d], list_sem, (d,), target[d]) for d in range(4)
    ]
    for copy in list_copies:
        copy.start()

    def psf_copy(k, index, device):
        return pltpu.make_async_remote_copy(
            src_ref=kp.at[k], dst_ref=kp.at[k],
            send_sem=psf_send.at[index], recv_sem=psf_recv.at[k],
            device_id=device, device_id_type=MESH,
        )

    def x_copy(step):
        return psf_copy(kind_k + z, step - 1, x_peer(step))

    def z_copy(step):
        return psf_copy(kind_k + z, n_x + step - 1, z_peer(step))

    def z_arrival(step):
        return psf_copy(kind_k + lax.rem(z + step, n_z), 0, z_peer(step))

    def y_copy(step):
        return psf_copy(kind_k + lax.rem(z + step, n_z), n_x + n_z + step, partner)

    def y_arrival(step):
        return psf_copy(n_z - kind_k + lax.rem(z + step, n_z), 0, partner)

    @pl.when(x == kind)
    def _():
        kp[kind_k + z] = psf[...]
        for step in range(1, n_x):
            x_copy(step).start()

    def psf_along_z():
        @pl.when(x != kind)
        def _():
            psf_copy(kind_k + z, 0, sibling).wait_recv()

        for step in range(1, n_z):
            z_copy(step).start()
        y_copy(0).start()

    def psf_along_y():
        for near in range(1, n_z // 2 + 1):
            for step in sorted({near, n_z - near}):
                z_arrival(step).wait_recv()
                y_copy(step).start()

    def psf_here():
        for step in range(n_z):
            y_arrival(step).wait_recv()

    def amp_copy(it, d):
        return send(amps.at[it], amps_in.at[it, d], amp_sem, (it, d), target[d])

    def vis_copy(it, d):
        rows = pl.ds(CAP * d, CAP)
        return send(vout.at[it, rows], vin.at[it, b, rows], vis_sem, (it, d), target[d])

    def fwd_copy(it, d, half):
        rows = pl.ds(CAP * d, CAP)
        return send(vin.at[it, half, rows], vin.at[it, half, rows], fwd_sem, (it, d), sibling)

    def mine_copy(half):
        return send(mq.at[1, half], mq.at[1, half], mine_sem, (0,), sibling)

    def home_copy(it):
        return send(hsend.at[it], hin.at[it], home_sem, (it,), sibling)

    def part_copy(it, d, half):
        rows = pl.ds(CAP * d, CAP)
        return send(gflat.at[it, half, rows], gin.at[it, rows], part_sem, (it, d), sibling)

    def back_copy(it, d):
        rows = pl.ds(CAP * d, CAP)
        return send(gsum.at[it, rows], gret.at[it, rows], back_sem, (it, d), origin[d])

    def gain_copy(it, d):
        return send(ga_send.at[it], ga_ret.at[it, d], gain_sem, (it, d), origin[d])

    for d in range(4):
        amp_copy(0, d).start()

    for d in range(4):
        row = lists8[d + 1 : d + 2, :]
        rank, _ = places(row)
        entries[pl.ds(CAP * d, CAP), :] = chosen(row, rank)
    pick = entries[...].astype(F32)
    pick_out[...] = pick
    pick_back[...] = pick.T.astype(BF16)

    for load in loads:
        load.wait()

    def send_visitors(it):
        def body(j, carry):
            cols = pl.ds(pl.multiple_of(j * 256, 256), 256)
            vout[it, :, cols] = dot(pick_out[...].astype(BF16), mq[it, b, :, cols]).astype(BF16)
            return carry

        lax.fori_loop(0, HALF // 256, body, 0)
        for d in range(4):
            vis_copy(it, d).start()

    send_visitors(0)

    psf_along_z()
    mf[...] = mq[0, b].astype(F32)
    if 2 * n_z < SLOTS:
        kp[2 * n_z : SLOTS] = jnp.zeros((SLOTS - 2 * n_z, 96, 128), BF16)

    step_col[...] = turned(mstep[...])
    slot0 = lists8[0:1, :]
    is_slot = jnp.where(slot0 == lax.broadcasted_iota(I32, (SLOTS, SRC), 0), 1.0, 0.0)
    bflat[...] = jnp.zeros(bflat.shape, BF16)
    pfx[0] = jnp.zeros((SIDE, 256), F32)
    pfx[65] = jnp.zeros((SIDE, 256), F32)

    for half in range(2):
        def obs_body(j, carry, half=half):
            cols = pl.ds(pl.multiple_of((half * 16 + j) * 128, 128), 128)
            parts = [obs[band, :, cols].astype(F32) for band in range(3)]
            to_stamps(parts, o_lo, o_hi, half * 16 + j)
            return carry

        tiled(16, ROWS, obs_body)

    def take_lists():
        table[...] = jnp.zeros((8, SRC), I32)
        for d in range(4):
            list_copies[d].wait_recv()
            row = lists_in[d, d + 1 : d + 2, :]
            rank, below = places(row)
            picked = chosen(row, rank)
            entries[pl.ds(CAP * d, CAP), :] = picked
            table[d + 2 : d + 3, :] = jnp.minimum(below, CAP)
        first, second = [], []
        for d in range(4):
            picked = entries[pl.ds(CAP * d, CAP), :]
            first.append(picked * lists_in[d, 0:1, :])
            second.append(picked * lists_in[d, d + 1 : d + 2, :])
        table[0:1, :] = jnp.minimum(
            jnp.sum(jnp.concatenate(first, axis=0).T, axis=0, keepdims=True), SLOTS - 1
        )
        table[1:2, :] = jnp.minimum(
            jnp.sum(jnp.concatenate(second, axis=0).T, axis=0, keepdims=True), SLOTS - 1
        )

    take_lists()

    def with_table(smem):
        copy = pltpu.make_async_copy(table, smem, table_sem)
        copy.start()
        copy.wait()
        for it in range(ITERS):
            one_iteration(it, smem)

    def home_weights(it):
        rows = [is_slot * amps[it, band : band + 1, :] for band in range(3)]
        full = jnp.concatenate(rows + [jnp.zeros((SRC - 48, SRC), F32)], axis=0)
        home_amp[...] = full[0:48].astype(BF16)
        home_back[...] = full.T.astype(BF16)

    def unpack(k):
        mask = lane_lo(SIDE)
        p01 = kp[k, 0:SIDE, :].astype(F32)
        fold = kp[k, SIDE:96, :].astype(F32)
        mask32 = lane_lo(32)
        p2 = jnp.concatenate(
            [jnp.where(mask32, fold, 0.0), jnp.where(mask32, swap(fold), 0.0)], axis=0
        )
        flip = jnp.concatenate([p01, p2], axis=0).T
        u, w = flip[0:SIDE], flip[SIDE:128]
        k3[k, :, 0:128] = p01.astype(BF16)
        k3[k, :, 128:256] = p2.astype(BF16)
        kt3[k, :, 0:128] = jnp.where(mask, u, swap(w)).astype(BF16)
        kt3[k, :, 128:256] = jnp.where(mask, swap(u), 0.0).astype(BF16)
        zero = jnp.zeros((SIDE, 128), BF16)
        p01s = swap(p01)
        kst_lo[k, 0:64, :] = jnp.where(mask, p01, 0.0).astype(BF16)
        kst_lo[k, 64:128, :] = jnp.where(mask, p01s, 0.0).astype(BF16)
        kst_lo[k, 128:192, :] = p2.astype(BF16)
        kst_lo[k, 192:256, :] = zero
        kst_hi[k, 0:64, :] = jnp.where(mask, 0.0, p01s).astype(BF16)
        kst_hi[k, 64:128, :] = jnp.where(mask, 0.0, p01).astype(BF16)
        kst_hi[k, 128:192, :] = swap(p2).astype(BF16)
        kst_hi[k, 192:256, :] = zero

    def one_iteration(it, smem):
        home_weights(it)

        for half in range(2):
            def sum_body(j, carry, half=half):
                cols = pl.ds(pl.multiple_of(j * 128, 128), 128)
                x = dot(home_amp[...], mq[it, half, :, cols])
                to_stamps([x[0:16], x[16:32], x[32:48]], s_lo, s_hi, half * 16 + j)
                return carry

            tiled(16, ROWS, sum_body)

        def home_forward():
            if it == 0:
                psf_here()

                def unpack_body(q, carry):
                    unpack(q)
                    return carry

                tiled(SLOTS, 4, unpack_body)

            def home_model(step, carry):
                slots = [step * HOME + u for u in range(HOME)]
                z = []
                for q in slots:
                    rows = pl.ds(pl.multiple_of(q * PITCH, 8), SIDE)
                    s = jnp.concatenate([s_lo[rows, :], s_hi[rows, :]], axis=1).astype(BF16)
                    kt = kt3[q]
                    z.append(dot(s, block_diag(kt[:, 0:128], kt[:, 128:256])).astype(BF16))
                for q, zq in zip(slots, z):
                    model[q] = dot(k3[q], block_diag(zq[:, 0:128], zq[:, 128:256]))
                return carry

            lax.fori_loop(0, SLOTS // HOME, home_model, 0)

        def visitors_in():
            for d in range(4):
                amp_copy(it, d).wait_recv()
                picked = entries[pl.ds(CAP * d, CAP), :].astype(F32)
                cols = [
                    jnp.sum(picked * amps_in[it, d, band : band + 1, :], axis=1, keepdims=True)
                    for band in range(3)
                ]
                mask = lane_lo(CAP)
                rows = pl.ds(CAP * d, CAP)
                arep[rows, 0:128] = jnp.where(mask, cols[0], cols[1])
                arep[rows, 128:256] = jnp.where(mask, cols[2], 0.0)

            for d in range(4):
                vis_copy(it, d).wait_recv()
                fwd_copy(it, d, b).start()
            for d in range(4):
                fwd_copy(it, d, other).wait_recv()
            for half in range(2):
                def stamp_body(j, carry, half=half):
                    cols = pl.ds(pl.multiple_of(j * 128, 128), 128)
                    mask = lane_lo(64)
                    xa = vin[it, half, 0:64, cols].astype(F32)
                    xb = vin[it, half, 64:128, cols].astype(F32)
                    pair = half * 16 + j
                    xs[pl.ds(2 * pair, 64, stride=PITCH), :] = jnp.where(mask, xa, swap(xb))
                    xs[pl.ds(2 * pair + 1, 64, stride=PITCH), :] = jnp.where(mask, swap(xa), xb)
                    return carry

                tiled(16, ROWS, stamp_body)

        if it == 0:
            psf_along_y()
            visitors_in()
            home_forward()
        else:
            home_forward()
            visitors_in()

        def visit_model(step, carry):
            acc = list(carry)
            blank = jnp.zeros((SIDE, 256), BF16)
            pairs = [step * PAIRS + u for u in range(PAIRS)]
            which = [[smem[0, p + 64 * side] for side in range(2)] for p in pairs]
            z = []
            for p, ks in zip(pairs, which):
                x = xs[pl.ds(pl.multiple_of(p * PITCH, 8), SIDE), :].astype(BF16)
                for side in range(2):
                    kt = kt3[ks[side]]
                    weights = jnp.concatenate([kt, blank] if side == 0 else [blank, kt], axis=0)
                    z.append(dot(x, weights).astype(BF16))
            for u, (p, ks) in enumerate(zip(pairs, which)):
                for side in range(2):
                    v = p + 64 * side
                    zv = z[2 * u + side]
                    zs[v] = zv
                    conv = dot(k3[ks[side]], block_diag(zv[:, 0:128], zv[:, 128:256]))
                    acc[side] = acc[side] + conv * arep[pl.ds(v, 1), :]
                    pfx[65 * side + p + 1] = acc[side]
            return tuple(acc)

        start = jnp.zeros((SIDE, 256), F32)
        lax.fori_loop(0, 64 // PAIRS, visit_model, (start, start))

        def residual(step, carry):
            for u in range(HOME // 2):
                q = step * (HOME // 2) + u
                total = model[q]
                for d in range(4):
                    base = (0, 32, 65, 97)[d]
                    total = total + (pfx[base + smem[d + 2, q + 1]] - pfx[base + smem[d + 2, q]])
                rows = pl.ds(pl.multiple_of(q * PITCH, 8), SIDE)
                seen = jnp.concatenate([o_lo[rows, :], o_hi[rows, :]], axis=1)
                res = (total - seen).astype(BF16)
                resid[q] = block_diag(res[:, 0:128], res[:, 128:256])
            return carry

        lax.fori_loop(0, SLOTS // (HOME // 2), residual, 0)

        def visit_back(step, carry):
            pairs = [step * PAIRS + u for u in range(PAIRS)]
            which = [[smem[0, p + 64 * side] for side in range(2)] for p in pairs]
            scaled = []
            for p, ks in zip(pairs, which):
                for side in range(2):
                    v = p + 64 * side
                    t = dot(kt3[ks[side]], resid[smem[1, v]])
                    ga_rows[pl.ds(v, 1), :] = jnp.sum(t * zs[v].astype(F32), axis=0, keepdims=True)
                    scaled.append((t * arep[pl.ds(v, 1), :]).astype(BF16))
            for u, (p, ks) in enumerate(zip(pairs, which)):
                gs[pl.ds(pl.multiple_of(p * PITCH, 8), SIDE), :] = dot(
                    scaled[2 * u], kst_lo[ks[0]]
                ) + dot(scaled[2 * u + 1], kst_hi[ks[1]])
            return carry

        def flatten(first):
            for half in range(2):
                def grad_body(j, carry, half=half):
                    pair = half * 16 + j
                    mask = lane_lo(32)
                    e = gs[pl.ds(first * PITCH + 2 * pair, 32, stride=PITCH), :]
                    o = gs[pl.ds(first * PITCH + 2 * pair + 1, 32, stride=PITCH), :]
                    cols = pl.ds(pl.multiple_of(j * 128, 128), 128)
                    gflat[it, half, first : first + 32, cols] = jnp.where(mask, e, swap(o)).astype(BF16)
                    gflat[it, half, 64 + first : 96 + first, cols] = jnp.where(
                        mask, swap(e), o
                    ).astype(BF16)
                    return carry

                tiled(16, ROWS, grad_body)

        def give_back(d):
            part_copy(it, d, other).wait_recv()
            rows = pl.ds(CAP * d, CAP)
            gsum[it, rows, :] = (
                gflat[it, b, rows, :].astype(F32) + gin[it, rows, :].astype(F32)
            ).astype(BF16)
            back_copy(it, d).start()

        lax.fori_loop(0, 32 // PAIRS, visit_back, 0)
        flatten(0)
        for d in (0, 2):
            part_copy(it, d, other).start()
        lax.fori_loop(32 // PAIRS, 64 // PAIRS, visit_back, 0)
        flatten(32)
        for d in (1, 3):
            part_copy(it, d, other).start()
        for d in (0, 2):
            give_back(d)
        select = jnp.where(
            lax.broadcasted_iota(I32, (8, 256), 1) // SIDE
            == lax.broadcasted_iota(I32, (8, 256), 0),
            1.0,
            0.0,
        )
        ga_send[it] = lax.dot_general(
            select, ga_rows[...], (((1,), (1,)), ((), ())),
            preferred_element_type=F32, precision=lax.Precision.HIGHEST,
        )
        for d in range(4):
            gain_copy(it, d).start()

        def home_back_body(step, carry):
            slots = [step * HOME + u for u in range(HOME)]
            turns = [dot(kt3[q], resid[q]).astype(BF16) for q in slots]
            for q, t in zip(slots, turns):
                rows = pl.ds(pl.multiple_of(q * PITCH, 8), SIDE)
                kk = k3[q]
                back = dot(t, block_diag(kk[:, 0:128], kk[:, 128:256]))
                b_lo[rows, :] = back[:, 0:128]
                b_hi[rows, :] = back[:, 128:256]
            return carry

        lax.fori_loop(0, SLOTS // HOME, home_back_body, 0)
        for d in (1, 3):
            give_back(d)

        for half in range(2):
            def flat_body(j, carry, half=half):
                pair = half * 16 + j
                mask = lane_lo(SLOTS)
                even = pl.ds(2 * pair, SLOTS, stride=PITCH)
                odd = pl.ds(2 * pair + 1, SLOTS, stride=PITCH)
                e0, o0, e2, o2 = b_lo[even, :], b_lo[odd, :], b_hi[even, :], b_hi[odd, :]
                x = jnp.concatenate(
                    [
                        jnp.where(mask, e0, swap(o0)),
                        jnp.where(mask, swap(e0), o0),
                        jnp.where(mask, e2, swap(o2)),
                    ],
                    axis=0,
                )
                bflat[half, 0:48, pl.ds(pl.multiple_of(j * 128, 128), 128)] = x.astype(BF16)
                return carry

            tiled(16, ROWS, flat_body)

        def home_grad(j, carry):
            cols = pl.ds(pl.multiple_of(j * 256, 256), 256)
            hsend[it, :, cols] = dot(home_back[...], bflat[other, :, cols]).astype(BF16)
            hown[:, cols] = dot(home_back[...], bflat[b, :, cols])
            return carry

        tiled(8, 4, home_grad)
        home_copy(it).start()

        def home_gain(j, carry):
            cols = pl.ds(pl.multiple_of(j * 256, 256), 256)
            for half in range(2):
                carry = carry + lax.dot_general(
                    bflat[half, 0:48, cols], mq[it, half, :, cols], (((1,), (1,)), ((), ())),
                    preferred_element_type=F32,
                )
            return carry

        gain = lax.fori_loop(0, HALF // 256, home_gain, jnp.zeros((48, SRC), F32))
        ga_home[...] = jnp.concatenate(
            [
                jnp.sum(is_slot * gain[16 * band : 16 * band + 16], axis=0, keepdims=True)
                for band in range(3)
            ]
            + [jnp.zeros((5, SRC), F32)],
            axis=0,
        )

        lane = lax.broadcasted_iota(I32, (8, SRC), 1) // CAP
        returned = jnp.zeros((8, SRC), F32)
        for d in range(4):
            gain_copy(it, d).wait_recv()
            returned = returned + jnp.where(lane == d, ga_ret[it, d], 0.0)
        gain = ga_home[...] + jnp.dot(
            returned, pick_out[...], preferred_element_type=F32, precision=lax.Precision.HIGHEST
        )
        amp_now[...] = amp_now[...] - sstep[...] * gain
        if it == 0:
            amp_now[...] = jnp.maximum(amp_now[...], 0.0)
            amps[1] = amp_now[...].astype(BF16).astype(F32)
            for d in range(4):
                amp_copy(1, d).start()
        else:
            for band in range(3):
                out_a[band] = amp_now[band : band + 1, :]
        home_copy(it).wait_recv()
        for d in range(4):
            back_copy(it, d).wait_recv()

        def update(j, carry):
            cols = pl.ds(pl.multiple_of(j * 128, 128), 128)
            grad = hown[:, cols] + hin[it, :, cols].astype(F32)
            grad = grad + dot(pick_back[...], gret[it, :, cols])
            fresh = mf[:, cols] - step_col[...] * grad
            if it == 0:
                fresh = jnp.maximum(fresh, 0.0)
                mf[:, cols] = fresh
                mq[1, b, :, cols] = fresh.astype(BF16)
            else:
                out_m[:, cols] = fresh
            return carry

        tiled(16, ROWS, update)
        if it == 0:
            send_visitors(1)
            mine_copy(b).start()
            mine_copy(other).wait_recv()

    pl.run_scoped(with_table, pltpu.SMEM((8, SRC), I32))

    for copy in list_copies:
        copy.wait_send()
    mine_copy(b).wait_send()
    for it in range(ITERS):
        home_copy(it).wait_send()
        for d in range(4):
            amp_copy(it, d).wait_send()
            vis_copy(it, d).wait_send()
            fwd_copy(it, d, b).wait_send()
            part_copy(it, d, other).wait_send()
            back_copy(it, d).wait_send()
            gain_copy(it, d).wait_send()

    @pl.when(x == kind)
    def _():
        for step in range(1, n_x):
            x_copy(step).wait_send()

    for step in range(1, n_z):
        z_copy(step).wait_send()
    for step in range(n_z):
        y_copy(step).wait_send()


def shards(morphology, sed_amps, slot_lists, morph_step, sed_step, psf_kernels, observed):
    n_ra, n_dec = lax.axis_size("ra"), lax.axis_size("dec")
    n_x = 4 if n_ra == 32 else 2
    vmem = pl.BlockSpec(memory_space=pltpu.VMEM)
    hbm = pl.BlockSpec(memory_space=pl.ANY)
    dma = pltpu.SemaphoreType.DMA
    scratch = [
        pltpu.VMEM((96, 128), F32),
        pltpu.VMEM((96, 128), BF16),
        pltpu.VMEM((3, SLOTS, 2 * HALF), BF16),
        pltpu.VMEM((SLOTS, 96, 128), BF16),
        pltpu.VMEM((SLOTS, SIDE, 256), BF16),
        pltpu.VMEM((SLOTS, SIDE, 256), BF16),
        pltpu.VMEM((SLOTS, 256, 128), BF16),
        pltpu.VMEM((SLOTS, 256, 128), BF16),
        pltpu.VMEM((8, SRC), I32),
        pltpu.VMEM((4, 8, SRC), I32),
        pltpu.VMEM((2, 8, SRC), F32),
        pltpu.VMEM((2, 4, 8, SRC), F32),
        pltpu.VMEM((8, SRC), F32),
        pltpu.VMEM((SRC, SRC), F32),
        pltpu.VMEM((SRC, SRC), BF16),
        pltpu.VMEM((48, SRC), BF16),
        pltpu.VMEM((SRC, SRC), BF16),
        pltpu.VMEM((SRC, SRC), F32),
        pltpu.VMEM((SRC, SRC), I32),
        pltpu.VMEM((8, SRC), I32),
        pltpu.VMEM((2, 2, SRC, HALF), BF16),
        pltpu.VMEM((SRC, HALF), F32),
        pltpu.VMEM((2, SRC, HALF), BF16),
        pltpu.VMEM((2, 2, SRC, HALF), BF16),
        pltpu.VMEM((64 * PITCH, 128), F32),
        pltpu.VMEM((SLOTS * PITCH, 128), F32),
        pltpu.VMEM((SLOTS * PITCH, 128), F32),
        pltpu.VMEM((SLOTS * PITCH, 128), F32),
        pltpu.VMEM((SLOTS * PITCH, 128), F32),
        pltpu.VMEM((SRC, SIDE, 256), BF16),
        pltpu.VMEM((130, SIDE, 256), F32),
        pltpu.VMEM((SLOTS, SIDE, 256), F32),
        pltpu.VMEM((SLOTS, 256, 256), BF16),
        pltpu.VMEM((SLOTS * PITCH, 128), F32),
        pltpu.VMEM((SLOTS * PITCH, 128), F32),
        pltpu.VMEM((2, SRC, HALF), BF16),
        pltpu.VMEM((64 * PITCH, 128), F32),
        pltpu.VMEM((2, 2, SRC, HALF), BF16),
        pltpu.VMEM((2, SRC, HALF), BF16),
        pltpu.VMEM((2, SRC, HALF), BF16),
        pltpu.VMEM((2, SRC, HALF), BF16),
        pltpu.VMEM((SRC, HALF), F32),
        pltpu.VMEM((2, SRC, HALF), BF16),
        pltpu.VMEM((2, SRC, HALF), BF16),
        pltpu.VMEM((SRC, 256), F32),
        pltpu.VMEM((SRC, 256), F32),
        pltpu.VMEM((2, 8, SRC), F32),
        pltpu.VMEM((2, 4, 8, SRC), F32),
        pltpu.VMEM((8, SRC), F32),
        dma((n_x + 2 * (n_ra // n_x),)), dma((SLOTS,)),
        dma((2, 4)), dma((2, 2, 4)), dma((2, 2, 4)), dma((2, 2, 4)), dma((2, 1)), dma((2, 2)),
        dma((2, 2, 4)), dma((2, 2, 4)), dma((2, 2, 4)), dma, dma((3,)),
    ]
    out_m, out_a = pl.pallas_call(
        functools.partial(deblend, n_ra, n_dec, n_x),
        out_shape=(
            jax.ShapeDtypeStruct((SRC, HALF), F32),
            jax.ShapeDtypeStruct((3, 1, SRC), F32),
        ),
        in_specs=[hbm] + [vmem] * 5 + [hbm],
        out_specs=(vmem, vmem),
        scratch_shapes=scratch,
        compiler_params=pltpu.CompilerParams(
            collective_id=0, has_side_effects=True, vmem_limit_bytes=60 * 1024 * 1024
        ),
        name="deblend",
    )(
        morphology[0, 0], sed_amps.reshape(3, 1, SRC), slot_lists.reshape(5, 1, SRC),
        morph_step[0], sed_step[0], psf_kernels.reshape(3, 2 * HALF), observed[0, 0],
    )
    out_m, out_a = jnp.maximum(out_m, 0.0), jnp.maximum(out_a, 0.0)
    return out_m[None, None], out_a.reshape(1, 1, 3, SRC)


def solution(mesh):
    in_specs = (
        P("ra", "dec", None, None),
        P("ra", "dec", "band", None),
        P("ra", "dec", None, None),
        P("ra", "dec", None),
        P("ra", "dec", None),
        P("band", "ra", None),
        P("ra", "dec", "band", None, None),
    )
    out_specs = (P("ra", "dec", None, "band"), P("ra", "dec", "band", None))
    return jax.shard_map(shards, mesh=mesh, in_specs=in_specs, out_specs=out_specs, check_vma=False)
```

```python
import functools
import jax
import jax.numpy as jnp
from jax import lax
from jax.experimental import pallas as pl
from jax.experimental.pallas import tpu as pltpu
from jax.sharding import PartitionSpec as P

SIDE = 64
KERN = 32
ITERS = 2
SLOTS = 16
CAP = 32
SRC = 128
HALF = 2048
PART = CAP // 2
BASE = (0, 33, 66, 99)
PITCH = 72
ROWS = 8
HOME = 8
QUADS = 8
MESH = pl.DeviceIdType.MESH
F32 = jnp.float32
BF16 = jnp.bfloat16
I32 = jnp.int32


def lane_lo(rows):
    return lax.broadcasted_iota(I32, (rows, 128), 1) < SIDE


def swap(value):
    return pltpu.roll(value, SIDE, axis=1)


def block_diag(first, second):
    low = jnp.where(lane_lo(SIDE), 1.0, 0.0).astype(BF16)
    high = jnp.where(lane_lo(SIDE), 0.0, 1.0).astype(BF16)
    zero = jnp.zeros((SIDE, 128), BF16)
    return jnp.concatenate(
        [
            jnp.concatenate([first * low, zero], axis=1),
            jnp.concatenate([first * high, zero], axis=1),
            jnp.concatenate([zero, second], axis=1),
            jnp.concatenate([zero, zero], axis=1),
        ],
        axis=0,
    )


def dot(a, b):
    return jnp.dot(a, b, preferred_element_type=F32)


def tiled(count, unroll, body):
    def steps(step, carry):
        for u in range(unroll):
            body(step * unroll + u, carry)
        return carry

    lax.fori_loop(0, count // unroll, steps, 0)


def turned(row):
    return jnp.broadcast_to(row, (SRC, SRC)).T


def places(row):
    source = lax.broadcasted_iota(I32, (1, SRC), 1)
    key_row = row * SRC + source
    column = turned(row)
    key_col = column * SRC + lax.broadcasted_iota(I32, (SRC, SRC), 0)
    rank = jnp.sum(jnp.where(key_col < key_row, 1, 0), axis=0, keepdims=True)
    below = jnp.sum(
        jnp.where(column < lax.broadcasted_iota(I32, (SRC, SRC), 1), 1, 0), axis=0, keepdims=True
    )
    return rank, below


def chosen(row, rank):
    entry = lax.broadcasted_iota(I32, (CAP, SRC), 0)
    return jnp.where(rank == entry, 1, 0) * jnp.where(row < SLOTS, 1, 0)


def to_stamps(parts, low_ref, high_ref, pair):
    x0, x1, x2 = parts
    mask = lane_lo(SLOTS)
    even, odd = pl.ds(2 * pair, SLOTS, stride=PITCH), pl.ds(2 * pair + 1, SLOTS, stride=PITCH)
    low_ref[even, :] = jnp.where(mask, x0, swap(x1))
    low_ref[odd, :] = jnp.where(mask, swap(x0), x1)
    high_ref[even, :] = jnp.where(mask, x2, 0.0)
    high_ref[odd, :] = jnp.where(mask, swap(x2), 0.0)


def deblend(
    n_ra, n_dec, n_x,
    morph, sed, lists, mstep, sstep, psf_in, obs_in,
    out_m, out_a,
    psf_f, psf, obs, kp, k3, kt3, kst_lo, kst_hi,
    lists8, lists_in, amps, amps_in, amp_now,
    pick_out, pick_back, home_amp, home_back, step_col, entries, table, smem,
    mq, mf, vout, vin, xs, s_lo, s_hi, o_lo, o_hi, zs, pfx, model, resid,
    b_lo, b_hi, bflat, gs, gflat, gsum, gin, gret, hown, hsend, hin,
    arep, ga_rows, ga_send, ga_ret, ga_home,
    psf_send, psf_recv, list_sem, amp_sem, vis_sem, fwd_sem, mine_sem, home_sem,
    part_sem, back_sem, gain_sem, table_sem, load_sem,
):
    r = lax.axis_index("ra")
    c = lax.axis_index("dec")
    b = lax.axis_index("band")
    other = 1 - b
    right, left = lax.rem(r + 1, n_ra), lax.rem(r + n_ra - 1, n_ra)
    up, down = lax.rem(c + 1, n_dec), lax.rem(c + n_dec - 1, n_dec)
    target = [(right, c, b), (left, c, b), (r, up, b), (r, down, b)]
    origin = [(left, c, b), (right, c, b), (r, down, b), (r, up, b)]
    sibling = (r, c, other)
    n_z = n_ra // n_x
    x, z = r // n_z, lax.rem(r, n_z)
    kind = lax.rem(c, 2)
    kind_k = kind * n_z
    partner = (r, c + 1 - 2 * kind, b)

    def send(src, dst, sems, index, device):
        return pltpu.make_async_remote_copy(
            src_ref=src, dst_ref=dst,
            send_sem=sems.at[(0,) + index], recv_sem=sems.at[(1,) + index],
            device_id=device, device_id_type=MESH,
        )

    def x_peer(step):
        return (lax.rem(x + step, n_x) * n_z + z, c, b)

    def z_peer(step):
        return (x * n_z + lax.rem(z + step, n_z), c, b)

    barrier = pltpu.get_barrier_semaphore()
    for device in (
        target
        + [sibling]
        + [x_peer(step) for step in range(1, n_x)]
        + [z_peer(step) for step in range(1, n_z)]
    ):
        pl.semaphore_signal(barrier, inc=1, device_id=device, device_id_type=MESH)
    loads = [
        pltpu.make_async_copy(morph.at[:, pl.ds(HALF * half, HALF)], mq.at[0, half], load_sem.at[half])
        for half in range(2)
    ] + [pltpu.make_async_copy(obs_in, obs, load_sem.at[2])]
    for load in loads:
        load.start()
    lists8[...] = jnp.full((8, SRC), SLOTS, I32)
    for d in range(5):
        lists8[d : d + 1, :] = lists[d]
    amp_now[...] = jnp.zeros((8, SRC), F32)
    for band in range(3):
        amp_now[band : band + 1, :] = sed[band]
    amps[0] = amp_now[...].astype(BF16).astype(F32)
    own = psf_in[...].astype(F32)
    for j in range(32):
        x0, x1 = own[0:1, 128 * j : 128 * j + 128], own[1:2, 128 * j : 128 * j + 128]
        psf_f[2 * j : 2 * j + 1, :] = jnp.where(lane_lo(1), x0, swap(x1))
        psf_f[2 * j + 1 : 2 * j + 2, :] = jnp.where(lane_lo(1), swap(x0), x1)
    for j in range(16):
        x0 = own[2:3, 128 * j : 128 * j + 128]
        x1 = own[2:3, HALF + 128 * j : HALF + 128 * j + 128]
        psf_f[64 + 2 * j : 65 + 2 * j, :] = jnp.where(lane_lo(1), x0, swap(x1))
        psf_f[65 + 2 * j : 66 + 2 * j, :] = jnp.where(lane_lo(1), swap(x0), x1)
    psf[...] = psf_f[...].astype(BF16)
    pl.semaphore_wait(barrier, 5 + n_x - 1 + n_z - 1)

    list_copies = [
        send(lists8, lists_in.at[d], list_sem, (d,), target[d]) for d in range(4)
    ]
    for copy in list_copies:
        copy.start()

    def psf_copy(k, index, device):
        return pltpu.make_async_remote_copy(
            src_ref=kp.at[k], dst_ref=kp.at[k],
            send_sem=psf_send.at[index], recv_sem=psf_recv.at[k],
            device_id=device, device_id_type=MESH,
        )

    def x_copy(step):
        return psf_copy(kind_k + z, step - 1, x_peer(step))

    def z_copy(step):
        return psf_copy(kind_k + z, n_x + step - 1, z_peer(step))

    def z_arrival(step):
        return psf_copy(kind_k + lax.rem(z + step, n_z), 0, z_peer(step))

    def y_copy(step):
        return psf_copy(kind_k + lax.rem(z + step, n_z), n_x + n_z + step, partner)

    def y_arrival(step):
        return psf_copy(n_z - kind_k + lax.rem(z + step, n_z), 0, partner)

    @pl.when(x == kind)
    def _():
        kp[kind_k + z] = psf[...]
        for step in range(1, n_x):
            x_copy(step).start()

    def psf_along_z():
        @pl.when(x != kind)
        def _():
            psf_copy(kind_k + z, 0, sibling).wait_recv()

        for step in range(1, n_z):
            z_copy(step).start()
        y_copy(0).start()

    def psf_along_y():
        for near in range(1, n_z // 2 + 1):
            for step in sorted({near, n_z - near}):
                z_arrival(step).wait_recv()
                y_copy(step).start()

    def psf_here():
        for step in range(n_z):
            y_arrival(step).wait_recv()

    def amp_copy(it, d):
        return send(amps.at[it], amps_in.at[it, d], amp_sem, (it, d), target[d])

    def vis_copy(it, d, part):
        rows = pl.ds(CAP * d + PART * part, PART)
        return send(vout.at[it, rows], vin.at[it, b, rows], vis_sem, (it, d, part), target[d])

    def fwd_copy(it, d, part, half):
        rows = pl.ds(CAP * d + PART * part, PART)
        return send(vin.at[it, half, rows], vin.at[it, half, rows], fwd_sem, (it, d, part), sibling)

    def mine_copy(half):
        return send(mq.at[1, half], mq.at[1, half], mine_sem, (0,), sibling)

    def home_copy(it):
        return send(hsend.at[it], hin.at[it], home_sem, (it,), sibling)

    def part_copy(it, d, part, half):
        rows = pl.ds(CAP * d + PART * part, PART)
        return send(gflat.at[it, half, rows], gin.at[it, rows], part_sem, (it, d, part), sibling)

    def back_copy(it, d, part):
        rows = pl.ds(CAP * d + PART * part, PART)
        return send(gsum.at[it, rows], gret.at[it, rows], back_sem, (it, d, part), origin[d])

    def gain_copy(it, d):
        return send(ga_send.at[it], ga_ret.at[it, d], gain_sem, (it, d), origin[d])

    for d in range(4):
        amp_copy(0, d).start()

    for d in range(4):
        row = lists8[d + 1 : d + 2, :]
        rank, _ = places(row)
        entries[pl.ds(CAP * d, CAP), :] = chosen(row, rank)
    pick = entries[...].astype(F32)
    pick_out[...] = pick
    pick_back[...] = pick.T.astype(BF16)

    for load in loads:
        load.wait()

    def send_visitors(it):
        def body(j, carry):
            cols = pl.ds(pl.multiple_of(j * 256, 256), 256)
            vout[it, :, cols] = dot(pick_out[...].astype(BF16), mq[it, b, :, cols]).astype(BF16)
            return carry

        tiled(8, 8, body)
        for part in range(2):
            for d in range(4):
                vis_copy(it, d, part).start()

    send_visitors(0)

    psf_along_z()
    mf[...] = mq[0, b].astype(F32)
    if 2 * n_z < SLOTS:
        kp[2 * n_z : SLOTS] = jnp.zeros((SLOTS - 2 * n_z, 96, 128), BF16)

    step_col[...] = turned(mstep[...])
    slot0 = lists8[0:1, :]
    is_slot = jnp.where(slot0 == lax.broadcasted_iota(I32, (SLOTS, SRC), 0), 1.0, 0.0)
    bflat[...] = jnp.zeros(bflat.shape, BF16)
    pfx[0] = jnp.zeros((SIDE, 256), F32)
    for d in range(1, 4):
        pfx[BASE[d]] = jnp.zeros((SIDE, 256), F32)

    for half in range(2):
        def obs_body(j, carry, half=half):
            cols = pl.ds(pl.multiple_of((half * 16 + j) * 128, 128), 128)
            parts = [obs[band, :, cols].astype(F32) for band in range(3)]
            to_stamps(parts, o_lo, o_hi, half * 16 + j)
            return carry

        tiled(16, ROWS, obs_body)

    def take_lists():
        table[...] = jnp.zeros((8, SRC), I32)
        for d in range(4):
            list_copies[d].wait_recv()
            row = lists_in[d, d + 1 : d + 2, :]
            rank, below = places(row)
            picked = chosen(row, rank)
            entries[pl.ds(CAP * d, CAP), :] = picked
            table[d + 2 : d + 3, :] = jnp.minimum(below, CAP)
        first, second = [], []
        for d in range(4):
            picked = entries[pl.ds(CAP * d, CAP), :]
            first.append(picked * lists_in[d, 0:1, :])
            second.append(picked * lists_in[d, d + 1 : d + 2, :])
        table[0:1, :] = jnp.minimum(
            jnp.sum(jnp.concatenate(first, axis=0).T, axis=0, keepdims=True), SLOTS - 1
        )
        table[1:2, :] = jnp.minimum(
            jnp.sum(jnp.concatenate(second, axis=0).T, axis=0, keepdims=True), SLOTS - 1
        )
        copy = pltpu.make_async_copy(table, smem, table_sem)
        copy.start()
        copy.wait()

    def home_weights(it):
        rows = [is_slot * amps[it, band : band + 1, :] for band in range(3)]
        full = jnp.concatenate(rows + [jnp.zeros((SRC - 48, SRC), F32)], axis=0)
        home_amp[...] = full[0:48].astype(BF16)
        home_back[...] = full.T.astype(BF16)

    def unpack(k):
        mask = lane_lo(SIDE)
        p01 = kp[k, 0:SIDE, :].astype(F32)
        fold = kp[k, SIDE:96, :].astype(F32)
        mask32 = lane_lo(32)
        p2 = jnp.concatenate(
            [jnp.where(mask32, fold, 0.0), jnp.where(mask32, swap(fold), 0.0)], axis=0
        )
        flip = jnp.concatenate([p01, p2], axis=0).T
        u, w = flip[0:SIDE], flip[SIDE:128]
        k3[k, :, 0:128] = p01.astype(BF16)
        k3[k, :, 128:256] = p2.astype(BF16)
        kt3[k, :, 0:128] = jnp.where(mask, u, swap(w)).astype(BF16)
        kt3[k, :, 128:256] = jnp.where(mask, swap(u), 0.0).astype(BF16)
        zero = jnp.zeros((SIDE, 128), BF16)
        p01s = swap(p01)
        kst_lo[k, 0:64, :] = jnp.where(mask, p01, 0.0).astype(BF16)
        kst_lo[k, 64:128, :] = jnp.where(mask, p01s, 0.0).astype(BF16)
        kst_lo[k, 128:192, :] = p2.astype(BF16)
        kst_lo[k, 192:256, :] = zero
        kst_hi[k, 0:64, :] = jnp.where(mask, 0.0, p01s).astype(BF16)
        kst_hi[k, 64:128, :] = jnp.where(mask, 0.0, p01).astype(BF16)
        kst_hi[k, 128:192, :] = swap(p2).astype(BF16)
        kst_hi[k, 192:256, :] = zero

    def one_iteration(it):
        home_weights(it)

        for half in range(2):
            def sum_body(j, carry, half=half):
                cols = pl.ds(pl.multiple_of(j * 128, 128), 128)
                x = dot(home_amp[...], mq[it, half, :, cols])
                to_stamps([x[0:16], x[16:32], x[32:48]], s_lo, s_hi, half * 16 + j)
                return carry

            tiled(16, ROWS, sum_body)

        def home_convolved():
            if it == 0:
                psf_here()

                def unpack_body(q, carry):
                    unpack(q)
                    return carry

                tiled(SLOTS, 4, unpack_body)

            def home_model(step, carry):
                slots = [step * HOME + u for u in range(HOME)]
                z = []
                for q in slots:
                    rows = pl.ds(pl.multiple_of(q * PITCH, 8), SIDE)
                    s = jnp.concatenate([s_lo[rows, :], s_hi[rows, :]], axis=1).astype(BF16)
                    kt = kt3[q]
                    z.append(dot(s, block_diag(kt[:, 0:128], kt[:, 128:256])).astype(BF16))
                for q, zq in zip(slots, z):
                    model[q] = dot(k3[q], block_diag(zq[:, 0:128], zq[:, 128:256]))
                return carry

            lax.fori_loop(0, SLOTS // HOME, home_model, 0)

        def visitor_amps():
            for d in range(4):
                amp_copy(it, d).wait_recv()
                picked = entries[pl.ds(CAP * d, CAP), :].astype(F32)
                cols = [
                    jnp.sum(picked * amps_in[it, d, band : band + 1, :], axis=1, keepdims=True)
                    for band in range(3)
                ]
                mask = lane_lo(CAP)
                rows = pl.ds(CAP * d, CAP)
                arep[rows, 0:128] = jnp.where(mask, cols[0], cols[1])
                arep[rows, 128:256] = jnp.where(mask, cols[2], 0.0)

        def pass_on(part):
            for d in range(4):
                vis_copy(it, d, part).wait_recv()
                fwd_copy(it, d, part, b).start()

        def visitor_stamps(part):
            for d in range(4):
                fwd_copy(it, d, part, other).wait_recv()
            for half in range(2):
                def stamp_body(j, carry, half=half):
                    cols = pl.ds(pl.multiple_of(j * 128, 128), 128)
                    mask = lane_lo(PART)
                    pair = half * 16 + j
                    for first in (PART * part, CAP + PART * part):
                        xa = vin[it, half, first : first + PART, cols].astype(F32)
                        xb = vin[it, half, 64 + first : 64 + first + PART, cols].astype(F32)
                        row = first * PITCH + 2 * pair
                        xs[pl.ds(row, PART, stride=PITCH), :] = jnp.where(mask, xa, swap(xb))
                        xs[pl.ds(row + 1, PART, stride=PITCH), :] = jnp.where(mask, swap(xa), xb)
                    return carry

                tiled(16, ROWS, stamp_body)

        def visit_model(step, carry):
            blank = jnp.zeros((SIDE, 256), BF16)
            acc = [pfx[BASE[d] + step * QUADS] for d in range(4)]
            z = []
            for u in range(QUADS):
                p = step * QUADS + u
                for side in range(2):
                    row = pl.multiple_of((p + CAP * side) * PITCH, 8)
                    x = xs[pl.ds(row, SIDE), :].astype(BF16)
                    for d in (side, side + 2):
                        k = smem[0, CAP * d + p]
                        kt = kt3[k]
                        weights = jnp.concatenate([kt, blank] if d < 2 else [blank, kt], axis=0)
                        z.append((d, p, k, dot(x, weights).astype(BF16)))
            for d, p, k, zv in z:
                v = CAP * d + p
                zs[v] = zv
                conv = dot(k3[k], block_diag(zv[:, 0:128], zv[:, 128:256]))
                acc[d] = acc[d] + conv * arep[pl.ds(v, 1), :]
                pfx[BASE[d] + p + 1] = acc[d]
            return carry

        def visitors_modelled(part):
            steps = PART // QUADS
            lax.fori_loop(part * steps, (part + 1) * steps, visit_model, 0)

        if it == 0:
            take_lists()
            psf_along_y()
            visitor_amps()
            pass_on(0)
            pass_on(1)
            visitor_stamps(0)
            visitor_stamps(1)
            home_convolved()
        else:
            home_convolved()
            visitor_amps()
            pass_on(0)
            visitor_stamps(0)
            pass_on(1)
        visitors_modelled(0)
        if it > 0:
            visitor_stamps(1)
        visitors_modelled(1)

        def residual(step, carry):
            for u in range(HOME // 2):
                q = step * (HOME // 2) + u
                total = model[q]
                for d in range(4):
                    base = BASE[d]
                    total = total + (pfx[base + smem[d + 2, q + 1]] - pfx[base + smem[d + 2, q]])
                rows = pl.ds(pl.multiple_of(q * PITCH, 8), SIDE)
                seen = jnp.concatenate([o_lo[rows, :], o_hi[rows, :]], axis=1)
                res = (total - seen).astype(BF16)
                resid[q] = block_diag(res[:, 0:128], res[:, 128:256])
            return carry

        lax.fori_loop(0, SLOTS // (HOME // 2), residual, 0)

        def visit_back(step, carry):
            scaled = []
            for u in range(QUADS):
                p = step * QUADS + u
                for d in (0, 2, 1, 3):
                    v = CAP * d + p
                    k = smem[0, v]
                    t = dot(kt3[k], resid[smem[1, v]])
                    ga_rows[pl.ds(v, 1), :] = jnp.sum(t * zs[v].astype(F32), axis=0, keepdims=True)
                    scaled.append((k, (t * arep[pl.ds(v, 1), :]).astype(BF16)))
            for u in range(QUADS):
                for side in range(2):
                    p = step * QUADS + u + CAP * side
                    (ka, a), (kb, bb) = scaled[4 * u + 2 * side : 4 * u + 2 * side + 2]
                    gs[pl.ds(pl.multiple_of(p * PITCH, 8), SIDE), :] = dot(a, kst_lo[ka]) + dot(
                        bb, kst_hi[kb]
                    )
            return carry

        def flatten(part):
            for half in range(2):
                def grad_body(j, carry, half=half):
                    pair = half * 16 + j
                    mask = lane_lo(PART)
                    cols = pl.ds(pl.multiple_of(j * 128, 128), 128)
                    for first in (PART * part, CAP + PART * part):
                        row = first * PITCH + 2 * pair
                        e = gs[pl.ds(row, PART, stride=PITCH), :]
                        o = gs[pl.ds(row + 1, PART, stride=PITCH), :]
                        gflat[it, half, first : first + PART, cols] = jnp.where(
                            mask, e, swap(o)
                        ).astype(BF16)
                        gflat[it, half, 64 + first : 64 + first + PART, cols] = jnp.where(
                            mask, swap(e), o
                        ).astype(BF16)
                    return carry

                tiled(16, ROWS, grad_body)
            for d in range(4):
                part_copy(it, d, part, other).start()

        def give_back(part):
            for d in range(4):
                part_copy(it, d, part, other).wait_recv()
                rows = pl.ds(CAP * d + PART * part, PART)
                gsum[it, rows, :] = (
                    gflat[it, b, rows, :].astype(F32) + gin[it, rows, :].astype(F32)
                ).astype(BF16)
                back_copy(it, d, part).start()

        steps = PART // QUADS
        lax.fori_loop(0, steps, visit_back, 0)
        flatten(0)
        lax.fori_loop(steps, 2 * steps, visit_back, 0)
        flatten(1)
        give_back(0)
        select = jnp.where(
            lax.broadcasted_iota(I32, (8, 256), 1) // SIDE
            == lax.broadcasted_iota(I32, (8, 256), 0),
            1.0,
            0.0,
        )
        ga_send[it] = lax.dot_general(
            select, ga_rows[...], (((1,), (1,)), ((), ())),
            preferred_element_type=F32, precision=lax.Precision.HIGHEST,
        )
        for d in range(4):
            gain_copy(it, d).start()

        def home_back_body(step, carry):
            slots = [step * HOME + u for u in range(HOME)]
            turns = [dot(kt3[q], resid[q]).astype(BF16) for q in slots]
            for q, t in zip(slots, turns):
                rows = pl.ds(pl.multiple_of(q * PITCH, 8), SIDE)
                kk = k3[q]
                back = dot(t, block_diag(kk[:, 0:128], kk[:, 128:256]))
                b_lo[rows, :] = back[:, 0:128]
                b_hi[rows, :] = back[:, 128:256]
            return carry

        lax.fori_loop(0, SLOTS // HOME, home_back_body, 0)
        give_back(1)

        for half in range(2):
            def flat_body(j, carry, half=half):
                pair = half * 16 + j
                mask = lane_lo(SLOTS)
                even = pl.ds(2 * pair, SLOTS, stride=PITCH)
                odd = pl.ds(2 * pair + 1, SLOTS, stride=PITCH)
                e0, o0, e2, o2 = b_lo[even, :], b_lo[odd, :], b_hi[even, :], b_hi[odd, :]
                x = jnp.concatenate(
                    [
                        jnp.where(mask, e0, swap(o0)),
                        jnp.where(mask, swap(e0), o0),
                        jnp.where(mask, e2, swap(o2)),
                    ],
                    axis=0,
                )
                bflat[half, 0:48, pl.ds(pl.multiple_of(j * 128, 128), 128)] = x.astype(BF16)
                return carry

            tiled(16, ROWS, flat_body)

        def home_grad(j, carry):
            cols = pl.ds(pl.multiple_of(j * 256, 256), 256)
            hsend[it, :, cols] = dot(home_back[...], bflat[other, :, cols]).astype(BF16)
            hown[:, cols] = dot(home_back[...], bflat[b, :, cols])
            return carry

        tiled(8, 4, home_grad)
        home_copy(it).start()

        def home_gain(j, carry):
            terms = []
            for half in range(2):
                for u in range(2):
                    cols = pl.ds(pl.multiple_of(j * 1024 + u * 512, 512), 512)
                    terms.append(
                        lax.dot_general(
                            bflat[half, 0:48, cols], mq[it, half, :, cols],
                            (((1,), (1,)), ((), ())), preferred_element_type=F32,
                        )
                    )
            return carry + ((terms[0] + terms[1]) + (terms[2] + terms[3]))

        gain = lax.fori_loop(0, 2, home_gain, jnp.zeros((48, SRC), F32))
        ga_home[...] = jnp.concatenate(
            [
                jnp.sum(is_slot * gain[16 * band : 16 * band + 16], axis=0, keepdims=True)
                for band in range(3)
            ]
            + [jnp.zeros((5, SRC), F32)],
            axis=0,
        )

        lane = lax.broadcasted_iota(I32, (8, SRC), 1) // CAP
        returned = jnp.zeros((8, SRC), F32)
        for d in range(4):
            gain_copy(it, d).wait_recv()
            returned = returned + jnp.where(lane == d, ga_ret[it, d], 0.0)
        gain = ga_home[...] + jnp.dot(
            returned, pick_out[...], preferred_element_type=F32, precision=lax.Precision.HIGHEST
        )
        amp_now[...] = amp_now[...] - sstep[...] * gain
        if it == 0:
            amp_now[...] = jnp.maximum(amp_now[...], 0.0)
            amps[1] = amp_now[...].astype(BF16).astype(F32)
            for d in range(4):
                amp_copy(1, d).start()
        else:
            for band in range(3):
                out_a[band] = amp_now[band : band + 1, :]
        home_copy(it).wait_recv()
        for d in range(4):
            for part in range(2):
                back_copy(it, d, part).wait_recv()

        def update(j, carry):
            cols = pl.ds(pl.multiple_of(j * 128, 128), 128)
            grad = hown[:, cols] + hin[it, :, cols].astype(F32)
            grad = grad + dot(pick_back[...], gret[it, :, cols])
            fresh = mf[:, cols] - step_col[...] * grad
            if it == 0:
                fresh = jnp.maximum(fresh, 0.0)
                mf[:, cols] = fresh
                mq[1, b, :, cols] = fresh.astype(BF16)
            else:
                out_m[:, cols] = fresh
            return carry

        tiled(16, ROWS, update)
        if it == 0:
            send_visitors(1)
            mine_copy(b).start()
            mine_copy(other).wait_recv()

    for it in range(ITERS):
        one_iteration(it)

    for copy in list_copies:
        copy.wait_send()
    mine_copy(b).wait_send()
    for it in range(ITERS):
        home_copy(it).wait_send()
        for d in range(4):
            amp_copy(it, d).wait_send()
            for part in range(2):
                vis_copy(it, d, part).wait_send()
                fwd_copy(it, d, part, b).wait_send()
                part_copy(it, d, part, other).wait_send()
                back_copy(it, d, part).wait_send()
            gain_copy(it, d).wait_send()

    @pl.when(x == kind)
    def _():
        for step in range(1, n_x):
            x_copy(step).wait_send()

    for step in range(1, n_z):
        z_copy(step).wait_send()
    for step in range(n_z):
        y_copy(step).wait_send()


def shards(morphology, sed_amps, slot_lists, morph_step, sed_step, psf_kernels, observed):
    n_ra, n_dec = lax.axis_size("ra"), lax.axis_size("dec")
    n_x = 4 if n_ra == 32 else 2
    vmem = pl.BlockSpec(memory_space=pltpu.VMEM)
    hbm = pl.BlockSpec(memory_space=pl.ANY)
    dma = pltpu.SemaphoreType.DMA
    scratch = [
        pltpu.VMEM((96, 128), F32),
        pltpu.VMEM((96, 128), BF16),
        pltpu.VMEM((3, SLOTS, 2 * HALF), BF16),
        pltpu.VMEM((SLOTS, 96, 128), BF16),
        pltpu.VMEM((SLOTS, SIDE, 256), BF16),
        pltpu.VMEM((SLOTS, SIDE, 256), BF16),
        pltpu.VMEM((SLOTS, 256, 128), BF16),
        pltpu.VMEM((SLOTS, 256, 128), BF16),
        pltpu.VMEM((8, SRC), I32),
        pltpu.VMEM((4, 8, SRC), I32),
        pltpu.VMEM((2, 8, SRC), F32),
        pltpu.VMEM((2, 4, 8, SRC), F32),
        pltpu.VMEM((8, SRC), F32),
        pltpu.VMEM((SRC, SRC), F32),
        pltpu.VMEM((SRC, SRC), BF16),
        pltpu.VMEM((48, SRC), BF16),
        pltpu.VMEM((SRC, SRC), BF16),
        pltpu.VMEM((SRC, SRC), F32),
        pltpu.VMEM((SRC, SRC), I32),
        pltpu.VMEM((8, SRC), I32),
        pltpu.SMEM((8, SRC), I32),
        pltpu.VMEM((2, 2, SRC, HALF), BF16),
        pltpu.VMEM((SRC, HALF), F32),
        pltpu.VMEM((2, SRC, HALF), BF16),
        pltpu.VMEM((2, 2, SRC, HALF), BF16),
        pltpu.VMEM((64 * PITCH, 128), F32),
        pltpu.VMEM((SLOTS * PITCH, 128), F32),
        pltpu.VMEM((SLOTS * PITCH, 128), F32),
        pltpu.VMEM((SLOTS * PITCH, 128), F32),
        pltpu.VMEM((SLOTS * PITCH, 128), F32),
        pltpu.VMEM((SRC, SIDE, 256), BF16),
        pltpu.VMEM((132, SIDE, 256), F32),
        pltpu.VMEM((SLOTS, SIDE, 256), F32),
        pltpu.VMEM((SLOTS, 256, 256), BF16),
        pltpu.VMEM((SLOTS * PITCH, 128), F32),
        pltpu.VMEM((SLOTS * PITCH, 128), F32),
        pltpu.VMEM((2, SRC, HALF), BF16),
        pltpu.VMEM((64 * PITCH, 128), F32),
        pltpu.VMEM((2, 2, SRC, HALF), BF16),
        pltpu.VMEM((2, SRC, HALF), BF16),
        pltpu.VMEM((2, SRC, HALF), BF16),
        pltpu.VMEM((2, SRC, HALF), BF16),
        pltpu.VMEM((SRC, HALF), F32),
        pltpu.VMEM((2, SRC, HALF), BF16),
        pltpu.VMEM((2, SRC, HALF), BF16),
        pltpu.VMEM((SRC, 256), F32),
        pltpu.VMEM((SRC, 256), F32),
        pltpu.VMEM((2, 8, SRC), F32),
        pltpu.VMEM((2, 4, 8, SRC), F32),
        pltpu.VMEM((8, SRC), F32),
        dma((n_x + 2 * (n_ra // n_x),)), dma((SLOTS,)),
        dma((2, 4)), dma((2, 2, 4)), dma((2, 2, 4, 2)), dma((2, 2, 4, 2)), dma((2, 1)), dma((2, 2)),
        dma((2, 2, 4, 2)), dma((2, 2, 4, 2)), dma((2, 2, 4)), dma, dma((3,)),
    ]
    out_m, out_a = pl.pallas_call(
        functools.partial(deblend, n_ra, n_dec, n_x),
        out_shape=(
            jax.ShapeDtypeStruct((SRC, HALF), F32),
            jax.ShapeDtypeStruct((3, 1, SRC), F32),
        ),
        in_specs=[hbm] + [vmem] * 5 + [hbm],
        out_specs=(vmem, vmem),
        scratch_shapes=scratch,
        compiler_params=pltpu.CompilerParams(
            collective_id=0, has_side_effects=True, vmem_limit_bytes=48 * 1024 * 1024
        ),
        name="deblend",
    )(
        morphology[0, 0], sed_amps.reshape(3, 1, SRC), slot_lists.reshape(5, 1, SRC),
        morph_step[0], sed_step[0], psf_kernels.reshape(3, 2 * HALF), observed[0, 0],
    )
    out_m, out_a = jnp.maximum(out_m, 0.0), jnp.maximum(out_a, 0.0)
    return out_m[None, None], out_a.reshape(1, 1, 3, SRC)


def solution(mesh):
    in_specs = (
        P("ra", "dec", None, None),
        P("ra", "dec", "band", None),
        P("ra", "dec", None, None),
        P("ra", "dec", None),
        P("ra", "dec", None),
        P("band", "ra", None),
        P("ra", "dec", "band", None, None),
    )
    out_specs = (P("ra", "dec", None, "band"), P("ra", "dec", "band", None))
    return jax.shard_map(shards, mesh=mesh, in_specs=in_specs, out_specs=out_specs, check_vma=False)
```

```python
import functools
import jax
import jax.numpy as jnp
from jax import lax
from jax.experimental import pallas as pl
from jax.experimental.pallas import tpu as pltpu
from jax.sharding import PartitionSpec as P

SIDE = 64
KERN = 32
ITERS = 2
SLOTS = 16
CAP = 32
SRC = 128
HALF = 2048
PART = CAP // 2
BASE = (0, 33, 66, 99)
PITCH = 72
ROWS = 8
HOME = 8
QUADS = 8
MESH = pl.DeviceIdType.MESH
F32 = jnp.float32
BF16 = jnp.bfloat16
I32 = jnp.int32


def lane_lo(rows):
    return lax.broadcasted_iota(I32, (rows, 128), 1) < SIDE


def swap(value):
    return pltpu.roll(value, SIDE, axis=1)


def block_diag(first, second):
    low = jnp.where(lane_lo(SIDE), 1.0, 0.0).astype(BF16)
    high = jnp.where(lane_lo(SIDE), 0.0, 1.0).astype(BF16)
    zero = jnp.zeros((SIDE, 128), BF16)
    return jnp.concatenate(
        [
            jnp.concatenate([first * low, zero], axis=1),
            jnp.concatenate([first * high, zero], axis=1),
            jnp.concatenate([zero, second], axis=1),
            jnp.concatenate([zero, zero], axis=1),
        ],
        axis=0,
    )


def dot(a, b):
    return jnp.dot(a, b, preferred_element_type=F32)


def tiled(count, unroll, body):
    def steps(step, carry):
        for u in range(unroll):
            body(step * unroll + u, carry)
        return carry

    lax.fori_loop(0, count // unroll, steps, 0)


def turned(row):
    return jnp.broadcast_to(row, (SRC, SRC)).T


def places(row):
    source = lax.broadcasted_iota(I32, (1, SRC), 1)
    key_row = row * SRC + source
    column = turned(row)
    key_col = column * SRC + lax.broadcasted_iota(I32, (SRC, SRC), 0)
    rank = jnp.sum(jnp.where(key_col < key_row, 1, 0), axis=0, keepdims=True)
    below = jnp.sum(
        jnp.where(column < lax.broadcasted_iota(I32, (SRC, SRC), 1), 1, 0), axis=0, keepdims=True
    )
    return rank, below


def chosen(row, rank):
    entry = lax.broadcasted_iota(I32, (CAP, SRC), 0)
    return jnp.where(rank == entry, 1, 0) * jnp.where(row < SLOTS, 1, 0)


def to_stamps(parts, low_ref, high_ref, pair):
    x0, x1, x2 = parts
    mask = lane_lo(SLOTS)
    even, odd = pl.ds(2 * pair, SLOTS, stride=PITCH), pl.ds(2 * pair + 1, SLOTS, stride=PITCH)
    low_ref[even, :] = jnp.where(mask, x0, swap(x1))
    low_ref[odd, :] = jnp.where(mask, swap(x0), x1)
    high_ref[even, :] = jnp.where(mask, x2, 0.0)
    high_ref[odd, :] = jnp.where(mask, swap(x2), 0.0)


def deblend(
    n_ra, n_dec, n_x,
    morph, sed, lists, mstep, sstep, psf_in, obs_in,
    out_m, out_a,
    psf_f, psf, obs, kp, k3, kt3, kst_lo, kst_hi,
    lists8, lists_in, amps, amps_in, amp_now,
    pick_out, pick_back, home_amp, home_back, step_col, entries, table, smem,
    mq, mf, vout, vin, xs, s_lo, s_hi, o_lo, o_hi, zs, pfx, model, resid,
    b_lo, b_hi, bflat, gs, gflat, gsum, gin, gret, hown, hin, amps_twin, twin_back,
    arep, ga_rows, ga_send, ga_ret, ga_home,
    psf_send, psf_recv, list_sem, amp_sem, vis_sem, fwd_sem, mine_sem, home_sem,
    part_sem, back_sem, gain_sem, table_sem, load_sem, twin_sem,
):
    r = lax.axis_index("ra")
    c = lax.axis_index("dec")
    b = lax.axis_index("band")
    other = 1 - b
    right, left = lax.rem(r + 1, n_ra), lax.rem(r + n_ra - 1, n_ra)
    up, down = lax.rem(c + 1, n_dec), lax.rem(c + n_dec - 1, n_dec)
    target = [(right, c, b), (left, c, b), (r, up, b), (r, down, b)]
    origin = [(left, c, b), (right, c, b), (r, down, b), (r, up, b)]
    sibling = (r, c, other)
    n_z = n_ra // n_x
    x, z = r // n_z, lax.rem(r, n_z)
    kind = lax.rem(c, 2)
    kind_k = kind * n_z
    partner = (r, c + 1 - 2 * kind, b)

    def send(src, dst, sems, index, device):
        return pltpu.make_async_remote_copy(
            src_ref=src, dst_ref=dst,
            send_sem=sems.at[(0,) + index], recv_sem=sems.at[(1,) + index],
            device_id=device, device_id_type=MESH,
        )

    def x_peer(step):
        return (lax.rem(x + step, n_x) * n_z + z, c, b)

    def z_peer(step):
        return (x * n_z + lax.rem(z + step, n_z), c, b)

    barrier = pltpu.get_barrier_semaphore()
    for device in (
        target
        + [sibling]
        + [x_peer(step) for step in range(1, n_x)]
        + [z_peer(step) for step in range(1, n_z)]
    ):
        pl.semaphore_signal(barrier, inc=1, device_id=device, device_id_type=MESH)
    loads = [
        pltpu.make_async_copy(morph.at[:, pl.ds(HALF * half, HALF)], mq.at[0, half], load_sem.at[half])
        for half in range(2)
    ] + [pltpu.make_async_copy(obs_in, obs, load_sem.at[2])]
    for load in loads:
        load.start()
    lists8[...] = jnp.full((8, SRC), SLOTS, I32)
    for d in range(5):
        lists8[d : d + 1, :] = lists[d]
    amp_now[...] = jnp.zeros((8, SRC), F32)
    for band in range(3):
        amp_now[band : band + 1, :] = sed[band]
    amps[0] = amp_now[...].astype(BF16).astype(F32)
    own = psf_in[...].astype(F32)
    for j in range(32):
        x0, x1 = own[0:1, 128 * j : 128 * j + 128], own[1:2, 128 * j : 128 * j + 128]
        psf_f[2 * j : 2 * j + 1, :] = jnp.where(lane_lo(1), x0, swap(x1))
        psf_f[2 * j + 1 : 2 * j + 2, :] = jnp.where(lane_lo(1), swap(x0), x1)
    for j in range(16):
        x0 = own[2:3, 128 * j : 128 * j + 128]
        x1 = own[2:3, HALF + 128 * j : HALF + 128 * j + 128]
        psf_f[64 + 2 * j : 65 + 2 * j, :] = jnp.where(lane_lo(1), x0, swap(x1))
        psf_f[65 + 2 * j : 66 + 2 * j, :] = jnp.where(lane_lo(1), swap(x0), x1)
    psf[...] = psf_f[...].astype(BF16)
    pl.semaphore_wait(barrier, 5 + n_x - 1 + n_z - 1)

    list_copies = [
        send(lists8, lists_in.at[d], list_sem, (d,), target[d]) for d in range(4)
    ]
    for copy in list_copies:
        copy.start()

    def psf_copy(k, index, device):
        return pltpu.make_async_remote_copy(
            src_ref=kp.at[k], dst_ref=kp.at[k],
            send_sem=psf_send.at[index], recv_sem=psf_recv.at[k],
            device_id=device, device_id_type=MESH,
        )

    def x_copy(step):
        return psf_copy(kind_k + z, step - 1, x_peer(step))

    def z_copy(step):
        return psf_copy(kind_k + z, n_x + step - 1, z_peer(step))

    def z_arrival(step):
        return psf_copy(kind_k + lax.rem(z + step, n_z), 0, z_peer(step))

    def y_copy(step):
        return psf_copy(kind_k + lax.rem(z + step, n_z), n_x + n_z + step, partner)

    def y_arrival(step):
        return psf_copy(n_z - kind_k + lax.rem(z + step, n_z), 0, partner)

    @pl.when(x == kind)
    def _():
        kp[kind_k + z] = psf[...]
        for step in range(1, n_x):
            x_copy(step).start()

    def psf_along_z():
        @pl.when(x != kind)
        def _():
            psf_copy(kind_k + z, 0, sibling).wait_recv()

        for step in range(1, n_z):
            z_copy(step).start()
        y_copy(0).start()

    def psf_along_y():
        for near in range(1, n_z // 2 + 1):
            for step in sorted({near, n_z - near}):
                z_arrival(step).wait_recv()
                y_copy(step).start()

    def psf_here():
        for step in range(n_z):
            y_arrival(step).wait_recv()

    def amp_copy(it, d):
        return send(amps.at[it], amps_in.at[it, d], amp_sem, (it, d), target[d])

    def vis_copy(it, d, part):
        rows = pl.ds(CAP * d + PART * part, PART)
        return send(vout.at[it, rows], vin.at[it, b, rows], vis_sem, (it, d, part), target[d])

    def fwd_copy(it, d, part, half):
        rows = pl.ds(CAP * d + PART * part, PART)
        return send(vin.at[it, half, rows], vin.at[it, half, rows], fwd_sem, (it, d, part), sibling)

    def mine_copy(half):
        return send(mq.at[1, half], mq.at[1, half], mine_sem, (0,), sibling)

    def home_copy(it):
        rows = pl.ds(0, 48)
        return send(bflat.at[other, rows], hin.at[it, rows], home_sem, (it,), sibling)

    def twin_copy(it):
        return send(amps.at[it], amps_twin.at[it], twin_sem, (it,), sibling)

    def part_copy(it, d, part, half):
        rows = pl.ds(CAP * d + PART * part, PART)
        return send(gflat.at[it, half, rows], gin.at[it, rows], part_sem, (it, d, part), sibling)

    def back_copy(it, d, part):
        rows = pl.ds(CAP * d + PART * part, PART)
        return send(gsum.at[it, rows], gret.at[it, rows], back_sem, (it, d, part), origin[d])

    def gain_copy(it, d):
        return send(ga_send.at[it], ga_ret.at[it, d], gain_sem, (it, d), origin[d])

    for d in range(4):
        amp_copy(0, d).start()
    twin_copy(0).start()

    for d in range(4):
        row = lists8[d + 1 : d + 2, :]
        rank, _ = places(row)
        entries[pl.ds(CAP * d, CAP), :] = chosen(row, rank)
    pick = entries[...].astype(F32)
    pick_out[...] = pick
    pick_back[...] = pick.T.astype(BF16)

    for load in loads:
        load.wait()

    def send_visitors(it):
        def body(j, carry):
            cols = pl.ds(pl.multiple_of(j * 256, 256), 256)
            vout[it, :, cols] = dot(pick_out[...].astype(BF16), mq[it, b, :, cols]).astype(BF16)
            return carry

        tiled(8, 8, body)
        for part in range(2):
            for d in range(4):
                vis_copy(it, d, part).start()

    send_visitors(0)

    psf_along_z()
    mf[...] = mq[0, b].astype(F32)
    if 2 * n_z < SLOTS:
        kp[2 * n_z : SLOTS] = jnp.zeros((SLOTS - 2 * n_z, 96, 128), BF16)

    step_col[...] = turned(mstep[...])
    slot0 = lists8[0:1, :]
    is_slot = jnp.where(slot0 == lax.broadcasted_iota(I32, (SLOTS, SRC), 0), 1.0, 0.0)
    bflat[...] = jnp.zeros(bflat.shape, BF16)
    hin[:, 48:SRC, :] = jnp.zeros((2, SRC - 48, HALF), BF16)
    pfx[0] = jnp.zeros((SIDE, 256), F32)
    for d in range(1, 4):
        pfx[BASE[d]] = jnp.zeros((SIDE, 256), F32)

    for half in range(2):
        def obs_body(j, carry, half=half):
            cols = pl.ds(pl.multiple_of((half * 16 + j) * 128, 128), 128)
            parts = [obs[band, :, cols].astype(F32) for band in range(3)]
            to_stamps(parts, o_lo, o_hi, half * 16 + j)
            return carry

        tiled(16, ROWS, obs_body)

    def take_lists():
        table[...] = jnp.zeros((8, SRC), I32)
        for d in range(4):
            list_copies[d].wait_recv()
            row = lists_in[d, d + 1 : d + 2, :]
            rank, below = places(row)
            picked = chosen(row, rank)
            entries[pl.ds(CAP * d, CAP), :] = picked
            table[d + 2 : d + 3, :] = jnp.minimum(below, CAP)
        first, second = [], []
        for d in range(4):
            picked = entries[pl.ds(CAP * d, CAP), :]
            first.append(picked * lists_in[d, 0:1, :])
            second.append(picked * lists_in[d, d + 1 : d + 2, :])
        table[0:1, :] = jnp.minimum(
            jnp.sum(jnp.concatenate(first, axis=0).T, axis=0, keepdims=True), SLOTS - 1
        )
        table[1:2, :] = jnp.minimum(
            jnp.sum(jnp.concatenate(second, axis=0).T, axis=0, keepdims=True), SLOTS - 1
        )
        copy = pltpu.make_async_copy(table, smem, table_sem)
        copy.start()
        copy.wait()

    def home_weights(it):
        rows = [is_slot * amps[it, band : band + 1, :] for band in range(3)]
        full = jnp.concatenate(rows + [jnp.zeros((SRC - 48, SRC), F32)], axis=0)
        home_amp[...] = full[0:48].astype(BF16)
        home_back[...] = full.T.astype(BF16)

    def unpack(k):
        mask = lane_lo(SIDE)
        p01 = kp[k, 0:SIDE, :].astype(F32)
        fold = kp[k, SIDE:96, :].astype(F32)
        mask32 = lane_lo(32)
        p2 = jnp.concatenate(
            [jnp.where(mask32, fold, 0.0), jnp.where(mask32, swap(fold), 0.0)], axis=0
        )
        flip = jnp.concatenate([p01, p2], axis=0).T
        u, w = flip[0:SIDE], flip[SIDE:128]
        k3[k, :, 0:128] = p01.astype(BF16)
        k3[k, :, 128:256] = p2.astype(BF16)
        kt3[k, :, 0:128] = jnp.where(mask, u, swap(w)).astype(BF16)
        kt3[k, :, 128:256] = jnp.where(mask, swap(u), 0.0).astype(BF16)
        zero = jnp.zeros((SIDE, 128), BF16)
        p01s = swap(p01)
        kst_lo[k, 0:64, :] = jnp.where(mask, p01, 0.0).astype(BF16)
        kst_lo[k, 64:128, :] = jnp.where(mask, p01s, 0.0).astype(BF16)
        kst_lo[k, 128:192, :] = p2.astype(BF16)
        kst_lo[k, 192:256, :] = zero
        kst_hi[k, 0:64, :] = jnp.where(mask, 0.0, p01s).astype(BF16)
        kst_hi[k, 64:128, :] = jnp.where(mask, 0.0, p01).astype(BF16)
        kst_hi[k, 128:192, :] = swap(p2).astype(BF16)
        kst_hi[k, 192:256, :] = zero

    def one_iteration(it):
        home_weights(it)

        for half in range(2):
            def sum_body(j, carry, half=half):
                cols = pl.ds(pl.multiple_of(j * 128, 128), 128)
                x = dot(home_amp[...], mq[it, half, :, cols])
                to_stamps([x[0:16], x[16:32], x[32:48]], s_lo, s_hi, half * 16 + j)
                return carry

            tiled(16, ROWS, sum_body)

        def home_convolved():
            if it == 0:
                psf_here()

                def unpack_body(q, carry):
                    unpack(q)
                    return carry

                tiled(SLOTS, 4, unpack_body)

            def home_model(step, carry):
                slots = [step * HOME + u for u in range(HOME)]
                z = []
                for q in slots:
                    rows = pl.ds(pl.multiple_of(q * PITCH, 8), SIDE)
                    s = jnp.concatenate([s_lo[rows, :], s_hi[rows, :]], axis=1).astype(BF16)
                    kt = kt3[q]
                    z.append(dot(s, block_diag(kt[:, 0:128], kt[:, 128:256])).astype(BF16))
                for q, zq in zip(slots, z):
                    model[q] = dot(k3[q], block_diag(zq[:, 0:128], zq[:, 128:256]))
                return carry

            lax.fori_loop(0, SLOTS // HOME, home_model, 0)

        def visitor_amps():
            for d in range(4):
                amp_copy(it, d).wait_recv()
                picked = entries[pl.ds(CAP * d, CAP), :].astype(F32)
                cols = [
                    jnp.sum(picked * amps_in[it, d, band : band + 1, :], axis=1, keepdims=True)
                    for band in range(3)
                ]
                mask = lane_lo(CAP)
                rows = pl.ds(CAP * d, CAP)
                arep[rows, 0:128] = jnp.where(mask, cols[0], cols[1])
                arep[rows, 128:256] = jnp.where(mask, cols[2], 0.0)

        def pass_on(part):
            for d in range(4):
                vis_copy(it, d, part).wait_recv()
                fwd_copy(it, d, part, b).start()

        def visitor_stamps(part):
            for d in range(4):
                fwd_copy(it, d, part, other).wait_recv()
            for half in range(2):
                def stamp_body(j, carry, half=half):
                    cols = pl.ds(pl.multiple_of(j * 128, 128), 128)
                    mask = lane_lo(PART)
                    pair = half * 16 + j
                    for first in (PART * part, CAP + PART * part):
                        xa = vin[it, half, first : first + PART, cols].astype(F32)
                        xb = vin[it, half, 64 + first : 64 + first + PART, cols].astype(F32)
                        row = first * PITCH + 2 * pair
                        xs[pl.ds(row, PART, stride=PITCH), :] = jnp.where(mask, xa, swap(xb))
                        xs[pl.ds(row + 1, PART, stride=PITCH), :] = jnp.where(mask, swap(xa), xb)
                    return carry

                tiled(16, ROWS, stamp_body)

        def visit_model(step, carry):
            blank = jnp.zeros((SIDE, 256), BF16)
            acc = [pfx[BASE[d] + step * QUADS] for d in range(4)]
            z = []
            for u in range(QUADS):
                p = step * QUADS + u
                for side in range(2):
                    row = pl.multiple_of((p + CAP * side) * PITCH, 8)
                    x = xs[pl.ds(row, SIDE), :].astype(BF16)
                    for d in (side, side + 2):
                        k = smem[0, CAP * d + p]
                        kt = kt3[k]
                        weights = jnp.concatenate([kt, blank] if d < 2 else [blank, kt], axis=0)
                        z.append((d, p, k, dot(x, weights).astype(BF16)))
            for d, p, k, zv in z:
                v = CAP * d + p
                zs[v] = zv
                conv = dot(k3[k], block_diag(zv[:, 0:128], zv[:, 128:256]))
                acc[d] = acc[d] + conv * arep[pl.ds(v, 1), :]
                pfx[BASE[d] + p + 1] = acc[d]
            return carry

        def visitors_modelled(part):
            steps = PART // QUADS
            lax.fori_loop(part * steps, (part + 1) * steps, visit_model, 0)

        if it == 0:
            take_lists()
            psf_along_y()
            visitor_amps()
            pass_on(0)
            pass_on(1)
            visitor_stamps(0)
            visitor_stamps(1)
            home_convolved()
        else:
            home_convolved()
            visitor_amps()
            pass_on(0)
            visitor_stamps(0)
            pass_on(1)
        visitors_modelled(0)
        if it > 0:
            visitor_stamps(1)
        visitors_modelled(1)

        def residual(step, carry):
            for u in range(HOME // 2):
                q = step * (HOME // 2) + u
                total = model[q]
                for d in range(4):
                    base = BASE[d]
                    total = total + (pfx[base + smem[d + 2, q + 1]] - pfx[base + smem[d + 2, q]])
                rows = pl.ds(pl.multiple_of(q * PITCH, 8), SIDE)
                seen = jnp.concatenate([o_lo[rows, :], o_hi[rows, :]], axis=1)
                res = (total - seen).astype(BF16)
                resid[q] = block_diag(res[:, 0:128], res[:, 128:256])
            return carry

        lax.fori_loop(0, SLOTS // (HOME // 2), residual, 0)

        def visit_back(step, carry):
            scaled = []
            for u in range(QUADS):
                p = step * QUADS + u
                for d in (0, 2, 1, 3):
                    v = CAP * d + p
                    k = smem[0, v]
                    t = dot(kt3[k], resid[smem[1, v]])
                    ga_rows[pl.ds(v, 1), :] = jnp.sum(t * zs[v].astype(F32), axis=0, keepdims=True)
                    scaled.append((k, (t * arep[pl.ds(v, 1), :]).astype(BF16)))
            for u in range(QUADS):
                for side in range(2):
                    p = step * QUADS + u + CAP * side
                    (ka, a), (kb, bb) = scaled[4 * u + 2 * side : 4 * u + 2 * side + 2]
                    gs[pl.ds(pl.multiple_of(p * PITCH, 8), SIDE), :] = dot(a, kst_lo[ka]) + dot(
                        bb, kst_hi[kb]
                    )
            return carry

        def flatten(part):
            for half in range(2):
                def grad_body(j, carry, half=half):
                    pair = half * 16 + j
                    mask = lane_lo(PART)
                    cols = pl.ds(pl.multiple_of(j * 128, 128), 128)
                    for first in (PART * part, CAP + PART * part):
                        row = first * PITCH + 2 * pair
                        e = gs[pl.ds(row, PART, stride=PITCH), :]
                        o = gs[pl.ds(row + 1, PART, stride=PITCH), :]
                        gflat[it, half, first : first + PART, cols] = jnp.where(
                            mask, e, swap(o)
                        ).astype(BF16)
                        gflat[it, half, 64 + first : 64 + first + PART, cols] = jnp.where(
                            mask, swap(e), o
                        ).astype(BF16)
                    return carry

                tiled(16, ROWS, grad_body)
            for d in range(4):
                part_copy(it, d, part, other).start()

        def give_back(part):
            for d in range(4):
                part_copy(it, d, part, other).wait_recv()
                rows = pl.ds(CAP * d + PART * part, PART)
                gsum[it, rows, :] = (
                    gflat[it, b, rows, :].astype(F32) + gin[it, rows, :].astype(F32)
                ).astype(BF16)
                back_copy(it, d, part).start()

        steps = PART // QUADS
        lax.fori_loop(0, steps, visit_back, 0)
        flatten(0)
        lax.fori_loop(steps, 2 * steps, visit_back, 0)
        flatten(1)
        give_back(0)
        select = jnp.where(
            lax.broadcasted_iota(I32, (8, 256), 1) // SIDE
            == lax.broadcasted_iota(I32, (8, 256), 0),
            1.0,
            0.0,
        )
        ga_send[it] = lax.dot_general(
            select, ga_rows[...], (((1,), (1,)), ((), ())),
            preferred_element_type=F32, precision=lax.Precision.HIGHEST,
        )
        for d in range(4):
            gain_copy(it, d).start()

        def home_back_body(step, carry):
            slots = [step * HOME + u for u in range(HOME)]
            turns = [dot(kt3[q], resid[q]).astype(BF16) for q in slots]
            for q, t in zip(slots, turns):
                rows = pl.ds(pl.multiple_of(q * PITCH, 8), SIDE)
                kk = k3[q]
                back = dot(t, block_diag(kk[:, 0:128], kk[:, 128:256]))
                b_lo[rows, :] = back[:, 0:128]
                b_hi[rows, :] = back[:, 128:256]
            return carry

        lax.fori_loop(0, SLOTS // HOME, home_back_body, 0)
        give_back(1)

        for half in range(2):
            def flat_body(j, carry, half=half):
                pair = half * 16 + j
                mask = lane_lo(SLOTS)
                even = pl.ds(2 * pair, SLOTS, stride=PITCH)
                odd = pl.ds(2 * pair + 1, SLOTS, stride=PITCH)
                e0, o0, e2, o2 = b_lo[even, :], b_lo[odd, :], b_hi[even, :], b_hi[odd, :]
                x = jnp.concatenate(
                    [
                        jnp.where(mask, e0, swap(o0)),
                        jnp.where(mask, swap(e0), o0),
                        jnp.where(mask, e2, swap(o2)),
                    ],
                    axis=0,
                )
                bflat[half, 0:48, pl.ds(pl.multiple_of(j * 128, 128), 128)] = x.astype(BF16)
                return carry

            tiled(16, ROWS, flat_body)

        home_copy(it).start()

        def home_grad(j, carry):
            cols = pl.ds(pl.multiple_of(j * 256, 256), 256)
            hown[:, cols] = dot(home_back[...], bflat[b, :, cols])
            return carry

        tiled(8, 4, home_grad)
        twin_copy(it).wait_recv()
        rows = [is_slot * amps_twin[it, band : band + 1, :] for band in range(3)]
        twin_back[...] = (
            jnp.concatenate(rows + [jnp.zeros((SRC - 48, SRC), F32)], axis=0).T.astype(BF16)
        )

        def home_gain(j, carry):
            terms = []
            for half in range(2):
                for u in range(2):
                    cols = pl.ds(pl.multiple_of(j * 1024 + u * 512, 512), 512)
                    terms.append(
                        lax.dot_general(
                            bflat[half, 0:48, cols], mq[it, half, :, cols],
                            (((1,), (1,)), ((), ())), preferred_element_type=F32,
                        )
                    )
            return carry + ((terms[0] + terms[1]) + (terms[2] + terms[3]))

        gain = lax.fori_loop(0, 2, home_gain, jnp.zeros((48, SRC), F32))
        ga_home[...] = jnp.concatenate(
            [
                jnp.sum(is_slot * gain[16 * band : 16 * band + 16], axis=0, keepdims=True)
                for band in range(3)
            ]
            + [jnp.zeros((5, SRC), F32)],
            axis=0,
        )

        lane = lax.broadcasted_iota(I32, (8, SRC), 1) // CAP
        returned = jnp.zeros((8, SRC), F32)
        for d in range(4):
            gain_copy(it, d).wait_recv()
            returned = returned + jnp.where(lane == d, ga_ret[it, d], 0.0)
        gain = ga_home[...] + jnp.dot(
            returned, pick_out[...], preferred_element_type=F32, precision=lax.Precision.HIGHEST
        )
        amp_now[...] = amp_now[...] - sstep[...] * gain
        if it == 0:
            amp_now[...] = jnp.maximum(amp_now[...], 0.0)
            amps[1] = amp_now[...].astype(BF16).astype(F32)
            for d in range(4):
                amp_copy(1, d).start()
            twin_copy(1).start()
        else:
            for band in range(3):
                out_a[band] = amp_now[band : band + 1, :]
        home_copy(it).wait_recv()
        home_copy(it).wait_send()
        for d in range(4):
            for part in range(2):
                back_copy(it, d, part).wait_recv()

        def update(j, carry):
            cols = pl.ds(pl.multiple_of(j * 128, 128), 128)
            grad = hown[:, cols] + dot(twin_back[...], hin[it, :, cols])
            grad = grad + dot(pick_back[...], gret[it, :, cols])
            fresh = mf[:, cols] - step_col[...] * grad
            if it == 0:
                fresh = jnp.maximum(fresh, 0.0)
                mf[:, cols] = fresh
                mq[1, b, :, cols] = fresh.astype(BF16)
            else:
                out_m[:, cols] = fresh
            return carry

        tiled(16, ROWS, update)
        if it == 0:
            send_visitors(1)
            mine_copy(b).start()
            mine_copy(other).wait_recv()

    for it in range(ITERS):
        one_iteration(it)

    for copy in list_copies:
        copy.wait_send()
    mine_copy(b).wait_send()
    for it in range(ITERS):
        twin_copy(it).wait_send()
        for d in range(4):
            amp_copy(it, d).wait_send()
            for part in range(2):
                vis_copy(it, d, part).wait_send()
                fwd_copy(it, d, part, b).wait_send()
                part_copy(it, d, part, other).wait_send()
                back_copy(it, d, part).wait_send()
            gain_copy(it, d).wait_send()

    @pl.when(x == kind)
    def _():
        for step in range(1, n_x):
            x_copy(step).wait_send()

    for step in range(1, n_z):
        z_copy(step).wait_send()
    for step in range(n_z):
        y_copy(step).wait_send()


def shards(morphology, sed_amps, slot_lists, morph_step, sed_step, psf_kernels, observed):
    n_ra, n_dec = lax.axis_size("ra"), lax.axis_size("dec")
    n_x = 4 if n_ra == 32 else 2
    vmem = pl.BlockSpec(memory_space=pltpu.VMEM)
    hbm = pl.BlockSpec(memory_space=pl.ANY)
    dma = pltpu.SemaphoreType.DMA
    scratch = [
        pltpu.VMEM((96, 128), F32),
        pltpu.VMEM((96, 128), BF16),
        pltpu.VMEM((3, SLOTS, 2 * HALF), BF16),
        pltpu.VMEM((SLOTS, 96, 128), BF16),
        pltpu.VMEM((SLOTS, SIDE, 256), BF16),
        pltpu.VMEM((SLOTS, SIDE, 256), BF16),
        pltpu.VMEM((SLOTS, 256, 128), BF16),
        pltpu.VMEM((SLOTS, 256, 128), BF16),
        pltpu.VMEM((8, SRC), I32),
        pltpu.VMEM((4, 8, SRC), I32),
        pltpu.VMEM((2, 8, SRC), F32),
        pltpu.VMEM((2, 4, 8, SRC), F32),
        pltpu.VMEM((8, SRC), F32),
        pltpu.VMEM((SRC, SRC), F32),
        pltpu.VMEM((SRC, SRC), BF16),
        pltpu.VMEM((48, SRC), BF16),
        pltpu.VMEM((SRC, SRC), BF16),
        pltpu.VMEM((SRC, SRC), F32),
        pltpu.VMEM((SRC, SRC), I32),
        pltpu.VMEM((8, SRC), I32),
        pltpu.SMEM((8, SRC), I32),
        pltpu.VMEM((2, 2, SRC, HALF), BF16),
        pltpu.VMEM((SRC, HALF), F32),
        pltpu.VMEM((2, SRC, HALF), BF16),
        pltpu.VMEM((2, 2, SRC, HALF), BF16),
        pltpu.VMEM((64 * PITCH, 128), F32),
        pltpu.VMEM((SLOTS * PITCH, 128), F32),
        pltpu.VMEM((SLOTS * PITCH, 128), F32),
        pltpu.VMEM((SLOTS * PITCH, 128), F32),
        pltpu.VMEM((SLOTS * PITCH, 128), F32),
        pltpu.VMEM((SRC, SIDE, 256), BF16),
        pltpu.VMEM((132, SIDE, 256), F32),
        pltpu.VMEM((SLOTS, SIDE, 256), F32),
        pltpu.VMEM((SLOTS, 256, 256), BF16),
        pltpu.VMEM((SLOTS * PITCH, 128), F32),
        pltpu.VMEM((SLOTS * PITCH, 128), F32),
        pltpu.VMEM((2, SRC, HALF), BF16),
        pltpu.VMEM((64 * PITCH, 128), F32),
        pltpu.VMEM((2, 2, SRC, HALF), BF16),
        pltpu.VMEM((2, SRC, HALF), BF16),
        pltpu.VMEM((2, SRC, HALF), BF16),
        pltpu.VMEM((2, SRC, HALF), BF16),
        pltpu.VMEM((SRC, HALF), F32),
        pltpu.VMEM((2, SRC, HALF), BF16),
        pltpu.VMEM((2, 8, SRC), F32),
        pltpu.VMEM((SRC, SRC), BF16),
        pltpu.VMEM((SRC, 256), F32),
        pltpu.VMEM((SRC, 256), F32),
        pltpu.VMEM((2, 8, SRC), F32),
        pltpu.VMEM((2, 4, 8, SRC), F32),
        pltpu.VMEM((8, SRC), F32),
        dma((n_x + 2 * (n_ra // n_x),)), dma((SLOTS,)),
        dma((2, 4)), dma((2, 2, 4)), dma((2, 2, 4, 2)), dma((2, 2, 4, 2)), dma((2, 1)), dma((2, 2)),
        dma((2, 2, 4, 2)), dma((2, 2, 4, 2)), dma((2, 2, 4)), dma, dma((3,)), dma((2, 2)),
    ]
    out_m, out_a = pl.pallas_call(
        functools.partial(deblend, n_ra, n_dec, n_x),
        out_shape=(
            jax.ShapeDtypeStruct((SRC, HALF), F32),
            jax.ShapeDtypeStruct((3, 1, SRC), F32),
        ),
        in_specs=[hbm] + [vmem] * 5 + [hbm],
        out_specs=(vmem, vmem),
        scratch_shapes=scratch,
        compiler_params=pltpu.CompilerParams(
            collective_id=0, has_side_effects=True, vmem_limit_bytes=48 * 1024 * 1024
        ),
        name="deblend",
    )(
        morphology[0, 0], sed_amps.reshape(3, 1, SRC), slot_lists.reshape(5, 1, SRC),
        morph_step[0], sed_step[0], psf_kernels.reshape(3, 2 * HALF), observed[0, 0],
    )
    out_m, out_a = jnp.maximum(out_m, 0.0), jnp.maximum(out_a, 0.0)
    return out_m[None, None], out_a.reshape(1, 1, 3, SRC)


def solution(mesh):
    in_specs = (
        P("ra", "dec", None, None),
        P("ra", "dec", "band", None),
        P("ra", "dec", None, None),
        P("ra", "dec", None),
        P("ra", "dec", None),
        P("band", "ra", None),
        P("ra", "dec", "band", None, None),
    )
    out_specs = (P("ra", "dec", None, "band"), P("ra", "dec", "band", None))
    return jax.shard_map(shards, mesh=mesh, in_specs=in_specs, out_specs=out_specs, check_vma=False)
```
